32 devices in a mesh: shard: 2 (over core), context: 4 (over y, x), tensor: 4 (over z).
Axes of the slice: x: 2, y: 2, z: 4, core: 2. Of those that a mesh axis runs over, the one named last changes fastest.
Arguments:
- tokens: bfloat16 [2, 4, 256, 2048], P('shard', 'context', None, 'tensor'), may hold values from -6 to 6
- parents: int32 [2, 4], P('shard'), may hold values from -1 to 3, as said below
- routes: int32 [2, 4, 256, 8], P('shard', 'context'), may hold values from 0 to 63, all different within a row
- pair_order: int32 [2, 4, 2048], P('shard', 'context'), may hold values from 0 to 2047, each once within a row
- norm_attn: bfloat16 [2048], P(('shard', 'context')), may hold values from 0.5 to 1.5
- w_query: bfloat16 [2048, 2048], P(('shard', 'context'), 'tensor'), may hold values from -0.125 to 0.125
- w_key: bfloat16 [2048, 2048], P(('shard', 'context'), 'tensor'), may hold values from -0.125 to 0.125
- w_value: bfloat16 [2048, 2048], P(('shard', 'context'), 'tensor'), may hold values from -0.125 to 0.125
- q_gain: bfloat16 [16, 128], P('tensor', ('shard', 'context')), may hold values from 0.099609375 to 1.8984375
- k_gain: bfloat16 [16, 128], P('tensor', ('shard', 'context')), may hold values from 0.099609375 to 1.8984375
- w_out: bfloat16 [2048, 2048], P('tensor', ('shard', 'context')), may hold values from -1 to 1
- norm_moe: bfloat16 [2048], P(('shard', 'context')), may hold values from 0.5 to 1.5
- w_router: bfloat16 [2048, 64], P(('shard', 'context')), may hold values from -0.06591797 to 0.06591797
- w_gate: bfloat16 [64, 2048, 1024], P(('shard', 'context'), None, 'tensor'), may hold values from -0.125 to 0.125
- w_up: bfloat16 [64, 2048, 1024], P(('shard', 'context'), None, 'tensor'), may hold values from -0.125 to 0.125
- w_down: bfloat16 [64, 1024, 2048], P(('shard', 'context'), 'tensor'), may hold values from -4.5 to 4.5
- out_grad: bfloat16 [2, 4, 256, 2048], P('shard', 'context', None, 'tensor'), may hold values from -6 to 6
Outputs:
- mixed: bfloat16 [2, 4, 256, 2048], P('shard', 'context', None, 'tensor')
- tokens_grad: float32 [2, 4, 256, 2048], P('shard', 'context', None, 'tensor')
- norm_attn_grad: float32 [2048], P(('shard', 'context'))
- w_query_grad: float32 [2048, 2048], P(('shard', 'context'), 'tensor')
- w_key_grad: float32 [2048, 2048], P(('shard', 'context'), 'tensor')
- w_value_grad: float32 [2048, 2048], P(('shard', 'context'), 'tensor')
- q_gain_grad: float32 [16, 128], P('tensor', ('shard', 'context'))
- k_gain_grad: float32 [16, 128], P('tensor', ('shard', 'context'))
- w_out_grad: float32 [2048, 2048], P('tensor', ('shard', 'context'))
- norm_moe_grad: float32 [2048], P(('shard', 'context'))
- w_router_grad: float32 [2048, 64], P(('shard', 'context'))
- w_gate_grad: float32 [64, 2048, 1024], P(('shard', 'context'), None, 'tensor')
- w_up_grad: float32 [64, 2048, 1024], P(('shard', 'context'), None, 'tensor')
- w_down_grad: float32 [64, 1024, 2048], P(('shard', 'context'), 'tensor')
The draws below stay inside these ranges and needn't reach their ends.
Inputs may be any that keep to these rules, and one draw needn't show every extreme that they name: Each row is one tree over the 4 slots with a single root (-1); following parents from any slot reaches the root. `routes`: each token names 8 different experts. `pair_order`: each segment's row is a permutation of its pairs, listed token by token, choice by choice.
All inputs are finite; a program needn't handle non-finite values.
Results may differ from the reference program's by a relative error of at most 0.017.
Values may be sent and summed in bfloat16 or wider, within the bound.
No kernel may reach another device: no remote copies, remote signals or barrier semaphores. Data moves between devices by JAX's collectives and lax.ppermute only.
A program may use at most 320 MiB of HBM per device.

```python
import jax
import jax.numpy as jnp
from jax import lax

D = 2048
HEADS = 16
HD = 128
EXPERTS = 64
FF = 1024
TOP = 8
SEG = 256
SEG_DEV = 1
TREES = 2
SLOTS = 4
TRUNK = 3
CAP = 40
N_CONTEXT = 4


def one_tree(key):
    key_pick = jax.random.fold_in(key, 1)
    key_forced = jax.random.fold_in(key, 2)
    key_rank = jax.random.fold_in(key, 3)
    key_link = jax.random.fold_in(key, 4)
    slot_ids = jnp.arange(SLOTS, dtype=jnp.int32)
    chosen_dev = jax.random.randint(key_pick, (3,), 0, SEG_DEV).astype(jnp.int32)
    forced = jnp.array([0, N_CONTEXT // 2 * SEG_DEV, (N_CONTEXT - 1) * SEG_DEV], dtype=jnp.int32) + chosen_dev
    forced_score = jax.random.randint(key_forced, (3,), 0, 64).astype(jnp.int32) * 3 + jnp.arange(3, dtype=jnp.int32)
    forced_rank = jnp.argsort(jnp.argsort(forced_score, stable=True), stable=True).astype(jnp.int32)
    other_score = jax.random.randint(key_rank, (SLOTS,), 0, SLOTS).astype(jnp.int32) * SLOTS + slot_ids
    ranking = other_score + 3
    for forced_index in range(3):
        ranking = jnp.where(slot_ids == forced[forced_index], forced_rank[forced_index], ranking)
    visit = jnp.argsort(ranking, stable=True).astype(jnp.int32)
    linked = jax.random.randint(key_link, (SLOTS,), TRUNK - 1, jnp.maximum(slot_ids, TRUNK)).astype(jnp.int32)
    parent_place = jnp.where(slot_ids < TRUNK, slot_ids - 1, linked)
    parent_slot = jnp.where(parent_place >= 0, visit[jnp.maximum(parent_place, 0)], -1).astype(jnp.int32)
    return jnp.zeros(SLOTS, jnp.int32).at[visit].set(parent_slot)


def draw_parents(key, part):
    key = jax.random.fold_in(key, 11)
    rows = [one_tree(jax.random.fold_in(key, 100 + tree_index)) for tree_index in range(TREES)]
    return jnp.stack(rows, 0)


def shard_levels(rng, shape, shards, low, largest):
    def one(dim, parts):
        steps = jax.random.uniform(jax.random.fold_in(jax.random.fold_in(rng, 6), dim), (parts,), jnp.float32, low / len(shards), largest / len(shards))
        return jnp.repeat(jnp.exp(steps), shape[dim] // parts).reshape((-1,) + (1,) * (len(shape) - dim - 1))

    loudness = one(*shards[0])
    for cut in shards[1:]:
        loudness = loudness * one(*cut)
    return loudness


def distinct(key, rows, count, top, lift):
    order = jax.random.permutation(jax.random.fold_in(key, 1), count)
    pull = order
    for power in range(3):
        pull = pull * pull // count
    pull = pull * lift // count
    lots = jax.random.randint(jax.random.fold_in(key, 2), (rows, count), 0, 4096) + pull
    holders = jax.random.permutation(jax.random.fold_in(key, 3), rows)[jnp.arange(count) % rows]
    lots = jnp.where(jnp.arange(rows)[:, None] == holders[None, :], 1 << 14, lots)
    score = lots * count + jnp.arange(count)
    return lax.top_k(score.astype(jnp.int32), top)[1].astype(jnp.int32)


def gaussian(stream_key, dims, scale, reach, split=(), kind=jnp.bfloat16):
    factor_of = shard_levels(stream_key, dims, split, -0.22, 0.18) if split else 1.0
    values = jax.random.normal(stream_key, dims, jnp.float32) * scale * factor_of
    return jnp.minimum(jnp.maximum(values, -reach), reach).astype(kind)


def setup_inputs(seed: int = 0) -> dict:
    splits = jax.random.split(jax.random.key(seed), 18)
    return {
        "tokens": gaussian(splits[0], (TREES, SLOTS, SEG, D), 1.0, 6.0, ((0, 2), (1, 4), (3, 4))),
        "parents": draw_parents(jax.random.fold_in(splits[17], 71), 0),
        "routes": distinct(splits[2], TREES * SLOTS * SEG, EXPERTS, TOP, 1024).reshape((TREES, SLOTS, SEG, TOP)),
        "pair_order": jax.vmap(lambda own: jax.random.permutation(own, SEG * TOP))(jax.random.split(splits[3], TREES * SLOTS)).reshape((TREES, SLOTS, SEG * TOP)).astype(jnp.int32),
        "norm_attn": jnp.clip(1.0 + 0.1 * jax.random.normal(splits[4], (D,), jnp.float32), 0.5, 1.5).astype(jnp.bfloat16),
        "w_query": gaussian(splits[5], (D, D), D ** -0.5, 0.125, ((0, 8), (1, 4))),
        "w_key": gaussian(splits[6], (D, D), D ** -0.5, 0.125, ((0, 8), (1, 4))),
        "w_value": gaussian(splits[7], (D, D), D ** -0.5, 0.125, ((0, 8), (1, 4))),
        "q_gain": jnp.clip(1.0 + 0.18 * jax.random.normal(splits[8], (HEADS, HD), jnp.float32), 0.099609375, 1.8984375).astype(jnp.bfloat16),
        "k_gain": jnp.clip(1.0 + 0.18 * jax.random.normal(splits[9], (HEADS, HD), jnp.float32), 0.099609375, 1.8984375).astype(jnp.bfloat16),
        "w_out": gaussian(splits[10], (D, D), (D // 64) ** -0.5, 1.0, ((0, 4), (1, 8))),
        "norm_moe": jnp.clip(1.0 + 0.1 * jax.random.normal(splits[11], (D,), jnp.float32), 0.5, 1.5).astype(jnp.bfloat16),
        "w_router": gaussian(splits[12], (D, EXPERTS), 0.011, 0.06591797, ((0, 8),)),
        "w_gate": gaussian(splits[13], (EXPERTS, D, FF), D ** -0.5, 0.125, ((0, 8), (2, 4))),
        "w_up": gaussian(splits[14], (EXPERTS, D, FF), D ** -0.5, 0.125, ((0, 8), (2, 4))),
        "w_down": gaussian(splits[15], (EXPERTS, FF, D), 0.75, 4.5, ((0, 8), (1, 4))),
        "out_grad": gaussian(splits[16], (TREES, SLOTS, SEG, D), 1.0, 6.0, ((0, 2), (1, 4), (3, 4))),
    }


EPS = 1e-05
ROPE_BASE = 10000.0
NEG_FILL = -1e+30

@jax.custom_vjp
def low(v):
    return lax.optimization_barrier(v.astype(jnp.bfloat16)).astype(jnp.float32)

@jax.custom_vjp
def low_back(v):
    return v

def low_keep(v):
    return (low(v), None)

def low_pass(kept, grad):
    return (grad,)

def back_keep(v):
    return (v, None)

def back_low(kept, grad):
    return (low(grad),)
low.defvjp(low_keep, low_pass)
low_back.defvjp(back_keep, back_low)

def matmul_high(left, right):
    return jnp.dot(left, right, precision=lax.Precision.HIGHEST)

def tree_info(parent_row):
    slot_count = parent_row.shape[0]
    slot_ids = jnp.arange(slot_count, dtype=jnp.int32)

    def climb_step(step_index, state_pair):
        current, reachable = state_pair
        current = jnp.where(current >= 0, parent_row[jnp.maximum(current, 0)], -1).astype(jnp.int32)
        reachable = reachable | (current[:, None] == slot_ids[None, :])
        return (current, reachable)
    initial = (slot_ids, slot_ids[:, None] == slot_ids[None, :])
    current, reachable = lax.fori_loop(0, slot_count, climb_step, initial)
    depths = lax.optimization_barrier(jnp.sum(reachable.astype(jnp.int32), 1)) - 1
    return (reachable, depths)

def rope_tables(positions, head_dim):
    half_dim = head_dim // 2
    frequency = ROPE_BASE ** (-2.0 * jnp.arange(half_dim, dtype=jnp.float32) / head_dim)
    angles = positions.astype(jnp.float32)[:, None] * frequency[None, :]
    cosine = jnp.concatenate([jnp.cos(angles), jnp.cos(angles)], -1)
    sine_table = jnp.concatenate([jnp.sin(angles), jnp.sin(angles)], -1)
    return (cosine, sine_table)

def rotate(values, cosine, sine_table):
    half_dim = values.shape[-1] // 2
    turned = jnp.concatenate([-values[..., half_dim:], values[..., :half_dim]], -1)
    return values * cosine[:, None, :] + turned * sine_table[:, None, :]

def segment_mask(reach_rows, own_rows, seg_len):
    offsets = jnp.arange(seg_len, dtype=jnp.int32)
    causal = offsets[None, :] <= offsets[:, None]
    full_mask = reach_rows[:, None, :, None] & (~own_rows[:, None, :, None] | causal[None, :, None, :])
    return full_mask.reshape(reach_rows.shape[0] * seg_len, reach_rows.shape[1] * seg_len)

def slotting(route_dev, order_dev, expert_count, capacity):
    seg_dev, seg_len, top_count = route_dev.shape
    pair_count = seg_dev * seg_len * top_count
    chosen = route_dev.reshape(pair_count).astype(jnp.int32)
    priority = (jnp.arange(seg_dev, dtype=jnp.int32)[:, None] * (seg_len * top_count) + order_dev).reshape(pair_count).astype(jnp.int32)
    pair_at = jnp.zeros(pair_count, jnp.int32).at[priority].set(jnp.arange(pair_count, dtype=jnp.int32))
    sorted_expert = chosen[pair_at]
    one_hot = (sorted_expert[:, None] == jnp.arange(expert_count, dtype=jnp.int32)[None, :]).astype(jnp.int32)
    place_sorted = lax.optimization_barrier(jnp.sum(jnp.cumsum(one_hot, 0) * one_hot, 1)) - 1
    placed = place_sorted[priority]
    target = jnp.where(placed < capacity, placed * expert_count + chosen, capacity * expert_count).astype(jnp.int32)
    return jnp.full((capacity * expert_count,), -1, jnp.int32).at[target].set(jnp.arange(pair_count, dtype=jnp.int32), mode='drop')

def rms_scale(values):
    return lax.rsqrt(lax.optimization_barrier(jnp.mean(values * values, -1, keepdims=True)) + EPS)

def reference(tokens, parents, routes, pair_order, norm_attn, w_query, w_key, w_value, q_gain, k_gain, w_out, norm_moe, w_router, w_gate, w_up, w_down, out_grad):
    source_count = TREES * N_CONTEXT
    dev_rows = SEG_DEV * SEG
    tree_len = SLOTS * SEG
    reach_all, depth_all = jax.vmap(tree_info)(parents)
    positions = (depth_all[:, :, None] * SEG + jnp.arange(SEG, dtype=jnp.int32)[None, None, :]).reshape(-1)
    cosine, sine_table = rope_tables(positions, HD)
    own_slot = jnp.arange(SLOTS)[:, None] == jnp.arange(SLOTS)[None, :]
    pair_table = jax.vmap(lambda route_dev, order_dev: slotting(route_dev, order_dev, EXPERTS, CAP))(routes.reshape(source_count, SEG_DEV, SEG, TOP), pair_order.reshape(source_count, SEG_DEV, SEG * TOP))
    expert_pairs = pair_table.reshape(source_count, CAP, EXPERTS).transpose(2, 0, 1)
    pair_filled = expert_pairs >= 0
    pair_safe = jnp.maximum(expert_pairs, 0)
    pair_tokens = pair_safe // TOP
    source_ids = jnp.arange(source_count, dtype=jnp.int32)[None, :, None]
    route_hot = (routes.reshape(-1, TOP)[:, :, None] == jnp.arange(EXPERTS)[None, None, :]).astype(jnp.float32)
    tree_ids = jnp.repeat(jnp.arange(TREES, dtype=jnp.int32), HEADS)
    score_scale = HD ** (-0.5)

    def attend(operands):
        query_head, key_head, value_head, tree_id = operands
        key_mask = segment_mask(reach_all[tree_id], own_slot, SEG)
        scores = low_back(matmul_high(query_head, key_head.T)) * score_scale
        scores = jnp.where(key_mask, scores, NEG_FILL)
        row_peak = lax.optimization_barrier(jnp.max(scores, -1, keepdims=True))
        weights = jnp.exp(scores - row_peak)
        probabilities = weights / lax.optimization_barrier(jnp.sum(weights, -1, keepdims=True))
        return matmul_high(low(probabilities), value_head)

    def heads_first(values):
        return values.reshape(TREES, tree_len, HEADS, HD).transpose(0, 2, 1, 3).reshape(TREES * HEADS, tree_len, HD)

    def forward(hidden_arg, gain_attn, query_weight, key_weight, value_weight, gain_query, gain_key, out_weight, gain_moe, router_weight, gate_weight, up_weight, down_weight):
        hidden_in = hidden_arg.reshape(-1, D)
        normed = hidden_in * rms_scale(hidden_in)
        attn_in = low(normed * gain_attn)
        queries = low_back(matmul_high(attn_in, query_weight))
        key_proj = low_back(matmul_high(attn_in, key_weight))
        value_proj = low(low_back(matmul_high(attn_in, value_weight)))
        query_norm = (queries * rms_scale(queries) * gain_query.reshape(-1)).reshape(-1, HEADS, HD)
        key_norm = (key_proj * rms_scale(key_proj) * gain_key.reshape(-1)).reshape(-1, HEADS, HD)
        query_rot = low(rotate(query_norm, cosine, sine_table))
        key_rot = low(rotate(key_norm, cosine, sine_table))
        attended = lax.map(jax.checkpoint(attend), (heads_first(query_rot), heads_first(key_rot), heads_first(value_proj.reshape(-1, HEADS, HD)), tree_ids))
        attended = attended.reshape(TREES, HEADS, tree_len, HD).transpose(0, 2, 1, 3).reshape(-1, D)
        attended = low(low_back(attended))
        residual = hidden_in + low_back(matmul_high(attended, out_weight))
        moe_in = low(residual * rms_scale(residual) * gain_moe)
        logits = low_back(matmul_high(moe_in, router_weight))
        row_peak = lax.optimization_barrier(jnp.max(logits, -1, keepdims=True))
        exponent = jnp.exp(logits - row_peak)
        router_probs = exponent / lax.optimization_barrier(jnp.sum(exponent, -1, keepdims=True))
        gate_values = lax.optimization_barrier(jnp.sum(route_hot * router_probs[:, None, :], -1))
        source_rows = moe_in.reshape(source_count, dev_rows, D)
        source_gates = gate_values.reshape(source_count, dev_rows * TOP)

        def expert_step(unused, operands):
            token_ids, filled, gate_one, up_one, down_one = operands
            gathered = jax.vmap(lambda rows_one, ids_one: rows_one[ids_one])(source_rows, token_ids)
            gathered = jnp.where(filled[:, :, None], gathered, 0.0)
            gate_proj = low_back(jnp.einsum('scd,df->scf', gathered, gate_one, precision=lax.Precision.HIGHEST))
            up_proj = low_back(jnp.einsum('scd,df->scf', gathered, up_one, precision=lax.Precision.HIGHEST))
            activated = low(gate_proj * jax.nn.sigmoid(gate_proj) * up_proj)
            expert_out = low_back(jnp.einsum('scf,fd->scd', activated, down_one, precision=lax.Precision.HIGHEST))
            return (unused, expert_out)
        unused, outputs = lax.scan(jax.checkpoint(expert_step), None, (pair_tokens, pair_filled, gate_weight, up_weight, down_weight))
        slot_gates = jax.vmap(lambda gates_one, ids_one: gates_one[ids_one], in_axes=(0, 1), out_axes=1)(source_gates, pair_safe)
        slot_gates = jnp.where(pair_filled, slot_gates, 0.0)
        moe_total = jnp.zeros((source_count, dev_rows, D), jnp.float32).at[source_ids, pair_tokens].add(slot_gates[:, :, :, None] * outputs)
        return (residual + moe_total.reshape(-1, D)).reshape(hidden_arg.shape)
    inputs = [operand.astype(jnp.float32) for operand in (tokens, norm_attn, w_query, w_key, w_value, q_gain, k_gain, w_out, norm_moe, w_router, w_gate, w_up, w_down)]
    result, pull_back = jax.vjp(forward, *inputs)
    grads = pull_back(out_grad.astype(jnp.float32))
    return (result.astype(jnp.bfloat16), grads[0], grads[1], grads[2], grads[3], grads[4], grads[5], grads[6], grads[7], grads[8], grads[9], grads[10], grads[11], grads[12])
```

```python
import jax
import jax.numpy as jnp
from jax import lax
from jax.sharding import PartitionSpec as P

EPS = 1e-05
ROPE_BASE = 10000.0
NEG_FILL = -1e30
SH, CT, TS = "shard", "context", "tensor"
F32, BF16 = jnp.float32, jnp.bfloat16


def swap(value, axis, rel):
    count = lax.axis_size(axis)
    return lax.ppermute(value, axis, [(i, i ^ rel) for i in range(count)])


def around(value, axis):
    return [value] + [swap(value, axis, rel) for rel in range(1, lax.axis_size(axis))]


def gather_groups(value):
    blocks = around(value, CT)
    for rel in range(1, lax.axis_size(SH)):
        blocks = blocks + [swap(block, SH, rel) for block in blocks[: lax.axis_size(CT)]]
    return blocks


def in_order(blocks, index):
    ordered = []
    for place in range(len(blocks)):
        picked = blocks[place]
        for mine in range(1, len(blocks)):
            picked = jnp.where(index == mine, blocks[place ^ mine], picked)
        ordered.append(picked)
    return ordered


def gather_tensor(value, axis=1):
    return jnp.concatenate(in_order(around(value, TS), lax.axis_index(TS)), axis)


def place_rows(blocks, index):
    rows = blocks[0].shape[0]
    whole = jnp.zeros((rows * len(blocks),) + blocks[0].shape[1:], blocks[0].dtype)
    for rel, block in enumerate(blocks):
        whole = lax.dynamic_update_slice_in_dim(whole, block, (index ^ rel) * rows, 0)
    return whole


def stack_blocks(blocks):
    whole = jnp.zeros((len(blocks),) + blocks[0].shape, blocks[0].dtype)
    for rel, block in enumerate(blocks):
        whole = lax.dynamic_update_index_in_dim(whole, block, rel, 0)
    return whole


def low(value):
    return value.astype(BF16)


def wide(value):
    return value.astype(F32)


def dot(left, right, left_dim=1, right_dim=0):
    return lax.dot_general(
        left, right, (((left_dim,), (right_dim,)), ((), ())), preferred_element_type=F32
    )


def group_sum(stacked):
    context_count = lax.axis_size(CT)
    mine = stacked[:context_count]
    for rel in range(1, lax.axis_size(SH)):
        other = swap(stacked[rel * context_count : (rel + 1) * context_count], SH, rel)
        mine = (wide(mine) + wide(other)).astype(stacked.dtype)
    total = wide(mine[0])
    for rel in range(1, context_count):
        total = total + wide(swap(mine[rel], CT, rel))
    return total


def group_trade(stacked):
    shard_count, context_count = lax.axis_size(SH), lax.axis_size(CT)
    parts = [stacked[:context_count]]
    for rel in range(1, shard_count):
        parts.append(swap(stacked[rel * context_count : (rel + 1) * context_count], SH, rel))
    parts = jnp.stack(parts)
    by_context = [parts[:, 0]] + [swap(parts[:, rel], CT, rel) for rel in range(1, context_count)]
    return [by_context[c][s] for s in range(shard_count) for c in range(context_count)]


def tree_info(parent_row):
    slot_count = parent_row.shape[0]
    slot_ids = jnp.arange(slot_count, dtype=jnp.int32)
    reach = (parent_row[:, None] == slot_ids[None, :]) | (slot_ids[:, None] == slot_ids[None, :])
    span = 1
    while span < slot_count:
        reach = jnp.any(reach[:, :, None] & reach[None, :, :], 1)
        span *= 2
    depths = jnp.sum(reach.astype(jnp.int32), 1) - 1
    return (reach, depths)


def rope_tables(positions, head_dim):
    half_dim = head_dim // 2
    frequency = ROPE_BASE ** (-2.0 * jnp.arange(half_dim, dtype=F32) / head_dim)
    angles = positions.astype(F32)[:, None] * frequency[None, :]
    cosine = jnp.concatenate([jnp.cos(angles), jnp.cos(angles)], -1)
    sine_table = jnp.concatenate([jnp.sin(angles), jnp.sin(angles)], -1)
    return (cosine, sine_table)


def rotate(values, cosine, sine_table):
    half_dim = values.shape[-1] // 2
    turned = jnp.concatenate([-values[..., half_dim:], values[..., :half_dim]], -1)
    return values * cosine[:, None, :] + turned * sine_table[:, None, :]


def rms_scale(values):
    return lax.rsqrt(jnp.mean(values * values, -1, keepdims=True) + EPS)


def own_slots(codes, pair_count, first_expert, expert_dev, capacity):
    expert_ids = first_expert + jnp.arange(expert_dev, dtype=jnp.int32)
    hit = (codes // pair_count)[:, :, :, None] == expert_ids
    rank = jnp.sum(jnp.where(hit, (codes % pair_count)[:, :, :, None], 0), 2)
    routed = jnp.any(hit, 2)
    rank = jnp.where(routed, rank, pair_count).transpose(0, 2, 1)
    routed = routed.transpose(0, 2, 1)
    place = jnp.sum((rank[:, :, None, :] < rank[:, :, :, None]).astype(jnp.int32), -1)
    return jnp.where(routed & (place < capacity), place, -1)


def split_low(value):
    high = low(value)
    return [high, low(value - wide(high))]


def per_device(
    tokens,
    parents,
    routes,
    pair_order,
    norm_attn,
    w_query,
    w_key,
    w_value,
    q_gain,
    k_gain,
    w_out,
    norm_moe,
    w_router,
    w_gate,
    w_up,
    w_down,
    out_grad,
):
    shard_index, context_index, tensor_index = (lax.axis_index(a) for a in (SH, CT, TS))
    context_count, tensor_count = lax.axis_size(CT), lax.axis_size(TS)
    group_count = lax.axis_size(SH) * context_count
    group = shard_index * context_count + context_index
    seg_dev, seg_len, quarter = tokens.shape[1:]
    rows = seg_dev * seg_len
    model_width = quarter * tensor_count
    slice_width = norm_attn.shape[0]
    top_count = routes.shape[3]
    expert_count = w_router.shape[1]
    expert_dev = w_gate.shape[0]
    local_heads, head_dim = q_gain.shape[0], q_gain.shape[1] * group_count
    head_width = local_heads * head_dim
    capacity = tensor_count * (
        (5 * rows * top_count + 4 * expert_count * tensor_count - 1)
        // (4 * expert_count * tensor_count)
    )
    score_scale = head_dim ** (-0.5)

    gain_size = q_gain.size
    gain_rows = jnp.concatenate([q_gain.reshape(-1), k_gain.reshape(-1)])
    gain_rows = jnp.pad(gain_rows, (0, slice_width - 2 * gain_size))
    small = jnp.concatenate(
        [w_router, norm_attn[:, None], norm_moe[:, None], gain_rows[:, None]], 1
    )
    small = jnp.pad(small, ((0, 0), (0, 128 - small.shape[1])))
    packed = jnp.concatenate([w_query, w_key, w_value, small], 1)
    packed = place_rows(gather_groups(packed), group)
    qkv_weight = packed[:, : 3 * head_width]
    small = packed[:, 3 * head_width :]
    router_weight = small[:, :expert_count]
    gain_attn = wide(small[:, expert_count])
    gain_moe = wide(small[:, expert_count + 1])
    gains = small[:, expert_count + 2].reshape(group_count, slice_width)[:, : 2 * gain_size]
    gains = gains.reshape(group_count, 2, local_heads, -1).transpose(1, 2, 0, 3)
    gain_query_row, gain_key_row = wide(gains.reshape(2, head_width))

    codes = routes.reshape(rows, top_count) * (rows * top_count) + (
        jnp.arange(seg_dev, dtype=jnp.int32)[:, None] * (seg_len * top_count) + pair_order[0]
    ).reshape(rows, top_count)
    codes = jnp.stack(gather_groups(codes))
    slots = own_slots(codes, rows * top_count, group * expert_dev, expert_dev, capacity)
    choose = low(slots[:, :, None, :] == jnp.arange(capacity, dtype=jnp.int32)[:, None])
    choose = choose.reshape(group_count, expert_dev * capacity, rows)

    hidden_in = wide(gather_tensor(tokens.reshape(rows, quarter)))
    out_weight = place_rows(gather_groups(w_out.T), group)
    grad_output = gather_tensor(out_grad.reshape(rows, quarter))
    grad_blocks = stack_blocks(gather_groups(grad_output))

    reachable, depths = tree_info(parents[0])
    first_slot = context_index * seg_dev
    local_depth = lax.dynamic_slice_in_dim(depths, first_slot, seg_dev, 0)
    offsets = jnp.arange(seg_len, dtype=jnp.int32)
    positions = (local_depth[:, None] * seg_len + offsets[None, :]).reshape(rows)
    cosine, sine_table = rope_tables(positions, head_dim)
    reach_local = lax.dynamic_slice_in_dim(reachable, first_slot, seg_dev, 0)
    masks = []
    for rel in range(context_count):
        other_slot = (context_index ^ rel) * seg_dev
        seen = lax.dynamic_slice_in_dim(reach_local, other_slot, seg_dev, 1)
        seen = seen[:, None, :, None]
        if rel == 0:
            same = jnp.eye(seg_dev, dtype=bool)[:, None, :, None]
            seen = seen & (~same | (offsets[None, :] <= offsets[:, None])[None, :, None, :])
        masks.append(jnp.broadcast_to(seen, (seg_dev, seg_len, seg_dev, seg_len)).reshape(rows, rows))
    key_mask = jnp.concatenate(masks, 1)

    scale_attn = rms_scale(hidden_in)
    normed = hidden_in * scale_attn
    attn_in = low(normed * gain_attn)
    attn_slices = group_trade(
        jnp.stack(
            [
                lax.dynamic_slice_in_dim(attn_in, (group ^ rel) * slice_width, slice_width, 1)
                for rel in range(group_count)
            ]
        )
    )
    projected = dot(attn_in, qkv_weight)
    queries = projected[:, :head_width]
    key_proj = projected[:, head_width : 2 * head_width]
    value_low = low(projected[:, 2 * head_width :])
    squares = jnp.stack([jnp.sum(queries * queries, -1), jnp.sum(key_proj * key_proj, -1)])
    squares = sum(in_order(around(squares, TS), tensor_index))
    scales = lax.rsqrt(squares / model_width + EPS)[:, :, None]
    query_hat = queries * scales[0]
    key_hat = key_proj * scales[1]

    def turn(hat, gain):
        return low(rotate((hat * gain).reshape(rows, local_heads, head_dim), cosine, sine_table))

    query_heads = turn(query_hat, gain_query_row).transpose(1, 0, 2)
    key_rot = turn(key_hat, gain_key_row).reshape(rows, head_width)
    key_value = jnp.concatenate([key_rot, value_low], 1)
    key_value = jnp.concatenate(around(key_value, CT), 0)
    key_value = key_value.reshape(context_count * rows, 2, local_heads, head_dim)
    key_heads, value_heads = key_value.transpose(1, 2, 0, 3)

    def attend(operands):
        query_one, key_one, value_one = operands
        scores = dot(query_one, key_one, 1, 1) * score_scale
        scores = jnp.where(key_mask, scores, NEG_FILL)
        row_peak = jnp.max(scores, -1, keepdims=True)
        weights = jnp.exp(scores - row_peak)
        row_total = jnp.sum(weights, -1, keepdims=True)
        return (dot(low(weights / row_total), value_one), row_peak[:, 0] + jnp.log(row_total[:, 0]))

    attended, log_total = lax.map(attend, (query_heads, key_heads, value_heads))
    attended_low = low(attended.transpose(1, 0, 2).reshape(rows, head_width))
    attended_blocks = jnp.concatenate(gather_groups(attended_low), 0)

    def tensor_parts(value):
        return [
            lax.dynamic_slice_in_dim(value, (tensor_index ^ rel) * quarter, quarter, 1)
            for rel in range(tensor_count)
        ]

    def tensor_sum(parts):
        total = wide(parts[0])
        for rel in range(1, tensor_count):
            total = total + wide(swap(low(parts[rel]), TS, rel))
        return total

    attn_share = tensor_sum(tensor_parts(dot(attended_low, out_weight, 1, 1)))
    residual_share = wide(tokens.reshape(rows, quarter)) + attn_share
    residual = wide(gather_tensor(low(residual_share)))
    scale_moe = rms_scale(residual)
    normed_moe = residual * scale_moe
    moe_in = low(normed_moe * gain_moe)
    logits = dot(moe_in, router_weight)
    exponent = jnp.exp(logits - jnp.max(logits, -1, keepdims=True))
    router_probs = exponent / jnp.sum(exponent, -1, keepdims=True)

    sent = jnp.concatenate([moe_in] + split_low(router_probs), 1)
    blocks = stack_blocks(gather_groups(sent))
    batched = (((2,), (1,)), ((0,), (0,)))
    pair_shape = (group_count, expert_dev, capacity, -1)
    picked = low(lax.dot_general(choose, blocks, batched, preferred_element_type=F32))
    picked = picked.reshape(pair_shape)
    grad_rows = low(lax.dot_general(choose, grad_blocks, batched, preferred_element_type=F32))
    grad_rows = grad_rows.reshape(pair_shape)
    pair_rows = picked[..., :model_width]
    pair_probs = wide(picked[..., model_width:]).reshape(
        group_count, expert_dev, capacity, 2, expert_count
    )
    own_expert = (
        jnp.arange(expert_count, dtype=jnp.int32)[None, :]
        == (group * expert_dev + jnp.arange(expert_dev, dtype=jnp.int32))[:, None]
    )
    pair_gates = jnp.sum(
        jnp.where(own_expert[None, :, None, :], jnp.sum(pair_probs, 3), 0.0), -1, keepdims=True
    )

    def by_expert(left, right, spec):
        return jnp.einsum(spec, left, right, preferred_element_type=F32)

    into, onto = "gekd,edf->gekf", "gekf,edf->gekd"
    gate_proj = by_expert(pair_rows, w_gate, into)
    up_proj = by_expert(pair_rows, w_up, into)
    sigmoid_gate = jax.nn.sigmoid(gate_proj)
    silu_gate = gate_proj * sigmoid_gate
    activated = low(silu_gate * up_proj)
    act_raw = by_expert(grad_rows, w_down, "gekd,efd->gekf")
    pair_dots = jnp.sum(wide(activated) * act_raw, -1, keepdims=True)
    act_grad = act_raw * pair_gates
    gate_low = low(act_grad * up_proj * sigmoid_gate * (1.0 + gate_proj * (1.0 - sigmoid_gate)))
    up_low = low(act_grad * silu_gate)
    row_grads = low(by_expert(gate_low, w_gate, onto) + by_expert(up_low, w_up, onto))
    dots = jnp.where(own_expert[None, :, None, :], pair_dots, 0.0)
    returned = jnp.concatenate([row_grads] + split_low(dots), -1)
    returned = returned.reshape(group_count, expert_dev * capacity, -1)
    combine = (((1,), (1,)), ((0,), (0,)))
    row_partial = low(lax.dot_general(choose, returned, combine, preferred_element_type=F32))
    row_total = group_sum(row_partial)

    after_rows = row_total[0, 0] * 0.0
    act_gated = low(wide(activated) * pair_gates + after_rows)
    expert_out = low(by_expert(act_gated, w_down, "gekf,efd->gekd"))
    expert_out = expert_out.reshape(group_count, expert_dev * capacity, model_width)
    mixed_partial = low(lax.dot_general(choose, expert_out, combine, preferred_element_type=F32))
    mixed_share = tensor_sum(tensor_parts(group_sum(mixed_partial)))
    mixed_out = low(residual_share + mixed_share).reshape(tokens.shape)
    down_grad = by_expert(act_gated, grad_rows, "gekf,gekd->efd")
    gate_w_grad = by_expert(pair_rows, gate_low, "gekd,gekf->edf")
    up_w_grad = by_expert(pair_rows, up_low, "gekd,gekf->edf")

    row_low = low(row_total)
    parts = [
        jnp.concatenate([part, row_low[:, model_width:]], 1)
        for part in tensor_parts(row_low[:, :model_width])
    ]
    parts = [parts[0]] + [swap(parts[rel], TS, rel) for rel in range(1, tensor_count)]
    row_share = sum(wide(part[:, :quarter]) for part in parts)
    prob_grads = sum(wide(part[:, quarter:]) for part in in_order(parts, tensor_index))
    prob_grads = prob_grads[:, :expert_count] + prob_grads[:, expert_count:]
    logit_low = low(
        router_probs * (prob_grads - jnp.sum(prob_grads * router_probs, -1, keepdims=True))
    )
    logit_blocks = gather_groups(logit_low)
    router_share = lax.dynamic_slice_in_dim(router_weight, tensor_index * quarter, quarter, 0)
    moe_in_grad = wide(gather_tensor(low(row_share + dot(logit_low, router_share, 1, 1))))
    blocks_slice = lax.dynamic_slice_in_dim(blocks, group * slice_width, slice_width, 2)
    router_grad = dot(
        blocks_slice.reshape(group_count * rows, slice_width), jnp.concatenate(logit_blocks, 0), 0, 0
    )
    gain_moe_grad = jnp.sum(moe_in_grad * normed_moe, 0)
    normed_grad = moe_in_grad * gain_moe
    residual_grad = wide(grad_output) + scale_moe * (
        normed_grad - normed_moe * jnp.mean(normed_grad * normed_moe, -1, keepdims=True)
    )
    residual_low = low(residual_grad)

    residual_slices = group_trade(
        jnp.stack(
            [
                lax.dynamic_slice_in_dim(residual_low, (group ^ rel) * slice_width, slice_width, 1)
                for rel in range(group_count)
            ]
        )
    )
    out_w_grad = dot(attended_blocks, jnp.concatenate(residual_slices, 0), 0, 0)
    grad_heads = low(dot(residual_low, out_weight))
    grad_heads = grad_heads.reshape(rows, local_heads, head_dim).transpose(1, 0, 2)

    def attend_back(operands):
        query_one, key_one, value_one, grad_one, total_one = operands
        scores = dot(query_one, key_one, 1, 1) * score_scale
        scores = jnp.where(key_mask, scores, NEG_FILL)
        probabilities = jnp.exp(scores - total_one[:, None])
        prob_grad = dot(grad_one, value_one, 1, 1)
        value_grad = dot(low(probabilities), grad_one, 0, 0)
        score_grad = probabilities * (
            prob_grad - jnp.sum(probabilities * prob_grad, -1, keepdims=True)
        )
        score_low = low(score_grad * score_scale)
        return (dot(score_low, key_one), low(dot(score_low, query_one, 0, 0)), low(value_grad))

    query_grad, key_grad, value_grad = lax.map(
        attend_back, (query_heads, key_heads, value_heads, grad_heads, log_total)
    )
    key_value_grad = jnp.stack([key_grad, value_grad]).transpose(2, 0, 1, 3)
    key_value_grad = key_value_grad.reshape(context_count, rows, 2 * head_width)
    total = wide(key_value_grad[0])
    for rel in range(1, context_count):
        total = total + wide(swap(key_value_grad[rel], CT, rel))

    def turn_back(grad):
        return rotate(grad.reshape(rows, local_heads, head_dim), cosine, -sine_table).reshape(
            rows, head_width
        )

    query_norm_grad = turn_back(query_grad.transpose(1, 0, 2))
    key_norm_grad = turn_back(total[:, :head_width])
    gain_query_grad = jnp.sum(query_norm_grad * query_hat, 0)
    gain_key_grad = jnp.sum(key_norm_grad * key_hat, 0)
    query_hat_grad = query_norm_grad * gain_query_row
    key_hat_grad = key_norm_grad * gain_key_row
    inner = jnp.stack([jnp.sum(query_hat_grad * query_hat, -1), jnp.sum(key_hat_grad * key_hat, -1)])
    inner = sum(in_order(around(inner, TS), tensor_index))[:, :, None] / model_width
    query_low = low(scales[0] * (query_hat_grad - query_hat * inner[0]))
    key_low = low(scales[1] * (key_hat_grad - key_hat * inner[1]))
    qkv_low = jnp.concatenate([query_low, key_low, low(total[:, head_width:])], 1)
    qkv_blocks = jnp.concatenate(gather_groups(qkv_low), 0)
    attn_share = tensor_sum(tensor_parts(dot(qkv_low, qkv_weight, 1, 1)))
    qkv_w_grad = dot(jnp.concatenate(attn_slices, 0), qkv_blocks, 0, 0)
    hidden_share = wide(tokens.reshape(rows, quarter))
    normed_share = hidden_share * scale_attn
    normed_in_grad = attn_share * lax.dynamic_slice_in_dim(gain_attn, tensor_index * quarter, quarter)
    inner = jnp.sum(normed_in_grad * normed_share, -1)
    ends = jnp.concatenate([inner, jnp.sum(attn_share * normed_share, 0)])
    ends = in_order(around(ends, TS), tensor_index)
    inner = sum(end[:rows] for end in ends)[:, None] / model_width
    gain_attn_grad = jnp.concatenate([end[rows:] for end in ends])
    residual_grad_share = lax.dynamic_slice_in_dim(
        residual_grad, tensor_index * quarter, quarter, 1
    )
    tokens_grad = residual_grad_share + scale_attn * (normed_in_grad - normed_share * inner)

    gain_grads = jnp.stack([gain_query_grad, gain_key_grad]).reshape(
        2, local_heads, group_count, -1
    )
    gain_grads = gain_grads.transpose(2, 0, 1, 3).reshape(group_count, 2 * gain_size)
    vectors = jnp.concatenate(
        [
            gain_attn_grad.reshape(group_count, slice_width),
            gain_moe_grad.reshape(group_count, slice_width),
            gain_grads,
        ],
        1,
    )
    vectors = group_sum(
        jnp.concatenate(
            [
                lax.dynamic_slice_in_dim(vectors, group ^ rel, 1, 0)[:, None]
                for rel in range(group_count)
            ]
        )
    )[0]
    gain_grads = vectors[2 * slice_width :].reshape((2,) + q_gain.shape)
    return (
        mixed_out,
        tokens_grad.reshape(tokens.shape),
        vectors[:slice_width],
        qkv_w_grad[:, :head_width],
        qkv_w_grad[:, head_width : 2 * head_width],
        qkv_w_grad[:, 2 * head_width :],
        gain_grads[0],
        gain_grads[1],
        out_w_grad,
        vectors[slice_width : 2 * slice_width],
        router_grad,
        gate_w_grad,
        up_w_grad,
        down_grad,
    )


def solution(mesh):
    both = (SH, CT)
    rows = P(SH, CT, None, TS)
    pairs = P(SH, CT, None, None)
    vector, matrix, turned = P(both), P(both, TS), P(TS, both)
    up, down = P(both, None, TS), P(both, TS, None)
    return jax.shard_map(
        per_device,
        mesh=mesh,
        in_specs=(
            rows,
            P(SH, None),
            pairs,
            P(SH, CT, None),
            vector,
            matrix,
            matrix,
            matrix,
            turned,
            turned,
            turned,
            vector,
            P(both, None),
            up,
            up,
            down,
            rows,
        ),
        out_specs=(
            rows,
            rows,
            vector,
            matrix,
            matrix,
            matrix,
            turned,
            turned,
            turned,
            vector,
            P(both, None),
            up,
            up,
            down,
        ),
        check_vma=False,
    )
```

```python
import functools

import jax
import jax.numpy as jnp
from jax import lax
from jax.experimental import pallas as pl
from jax.experimental.pallas import tpu as pltpu
from jax.sharding import PartitionSpec as P

EPS = 1e-05
ROPE_BASE = 10000.0
NEG_FILL = -1e30
SH, CT, TS = "shard", "context", "tensor"
F32, BF16 = jnp.float32, jnp.bfloat16
CHUNK = 512
VMEM_BYTES = 58 * 2**20


def swap(value, axis, rel):
    count = lax.axis_size(axis)
    return lax.ppermute(value, axis, [(i, i ^ rel) for i in range(count)])


def around(value, axis):
    return [value] + [swap(value, axis, rel) for rel in range(1, lax.axis_size(axis))]


def gather_context(value, *middle):
    half = value.shape[0] // 2
    if lax.axis_size(CT) != 4 or half % 16:
        return around(value, CT)
    first, second = hold(swap(value, CT, 1), *middle), hold(swap(value, CT, 2), *middle)
    third = [swap(first[:half], CT, 2), swap(second[half:], CT, 1)]
    return [value, first, second, jnp.concatenate(third)]


def gather_groups(value, *middle):
    blocks = gather_context(value, *middle)
    for rel in range(1, lax.axis_size(SH)):
        blocks = blocks + [swap(block, SH, rel) for block in blocks[: lax.axis_size(CT)]]
    return blocks


def stack_far(blocks):
    far = [swap(jnp.stack(blocks), SH, rel) for rel in range(1, lax.axis_size(SH))]
    return blocks + [(one, place) for one in far for place in range(len(blocks))]


def plain(block):
    return block[0][block[1]] if isinstance(block, tuple) else block


def array_of(block):
    return block[0] if isinstance(block, tuple) else block


def block_spec(block, size, column):
    if isinstance(block, tuple):
        array, place = block
        return pl.BlockSpec((None, array.shape[1], size), lambda i: (place, 0, column))
    return pl.BlockSpec((block.shape[0], size), lambda i: (0, column))


def butterfly(value, axis):
    rel = 1
    while rel < lax.axis_size(axis):
        value = value + swap(value, axis, rel)
        rel *= 2
    return value


def double(value, axis):
    rel = 1
    while rel < lax.axis_size(axis):
        value = jnp.concatenate([value, swap(value, axis, rel)])
        rel *= 2
    return value


def in_order(blocks, index):
    ordered = []
    for place in range(len(blocks)):
        picked = blocks[place]
        for mine in range(1, len(blocks)):
            picked = jnp.where(index == mine, blocks[place ^ mine], picked)
        ordered.append(picked)
    return ordered


def place_rows(blocks, index):
    rows = blocks[0].shape[0]
    whole = jnp.zeros((rows * len(blocks),) + blocks[0].shape[1:], blocks[0].dtype)
    for rel, block in enumerate(blocks):
        whole = lax.dynamic_update_slice_in_dim(whole, block, (index ^ rel) * rows, 0)
    return whole


def low(value):
    return value.astype(BF16)


def wide(value):
    return value.astype(F32)


def hold_kernel(*refs):
    pass


def hold(value, *others):
    if not others:
        return value
    anywhere = pl.BlockSpec(memory_space=pl.ANY)
    return pl.pallas_call(
        hold_kernel,
        out_shape=jax.ShapeDtypeStruct(value.shape, value.dtype),
        in_specs=[anywhere] * (1 + len(others)),
        out_specs=anywhere,
        input_output_aliases={0: 0},
        cost_estimate=pl.CostEstimate(flops=0, bytes_accessed=0, transcendentals=0),
    )(value, *others)


def dot(left, right, left_dim=1, right_dim=0):
    return lax.dot_general(
        left, right, (((left_dim,), (right_dim,)), ((), ())), preferred_element_type=F32
    )


def joint(values, *others):
    first = hold(values[0], *values[1:], *others)
    return [first] + [hold(value, first) for value in values[1:]]


def core_sum(other, mine):
    came = [swap(block, SH, 1) for block in other]
    return [(block, one) for block, one in zip(mine, came)]


def add_up(blocks, cut=slice(None)):
    return sum(wide(block[cut]) for block in blocks)


def context_start(mine):
    half = mine[0][0].shape[0] // 2
    if len(mine) != 4 or half % 16:
        return [swap(low(add_up(blocks)), CT, rel) for rel, blocks in enumerate(mine) if rel]
    top, bottom = slice(0, half), slice(half, None)
    upper = [low(add_up(mine[1], top)), low(add_up(mine[3], top))]
    lower = [low(add_up(mine[2], bottom)), low(add_up(mine[3], bottom))]
    return [swap(jnp.stack(upper), CT, 1), swap(jnp.stack(lower), CT, 2)]


def context_end(mine, came, *middle):
    half = mine[0][0].shape[0] // 2
    if len(mine) != 4 or half % 16:
        return add_up(mine[0]) + sum(wide(block) for block in came)
    top, bottom = slice(0, half), slice(half, None)
    upper, lower = joint(came, *middle)
    pass_upper = low(add_up(mine[2], top) + wide(upper[1]))
    pass_lower = low(add_up(mine[1], bottom) + wide(lower[1]))
    upper = add_up(mine[0], top) + wide(upper[0]) + wide(swap(pass_upper, CT, 2))
    lower = add_up(mine[0], bottom) + wide(lower[0]) + wide(swap(pass_lower, CT, 1))
    return jnp.concatenate([upper, lower])


def trade_start(stacked, *middle):
    shard_count, context_count = lax.axis_size(SH), lax.axis_size(CT)
    parts = [stacked[:context_count]]
    for rel in range(1, shard_count):
        parts.append(swap(stacked[rel * context_count : (rel + 1) * context_count], SH, rel))
    parts = jnp.stack(parts)
    return [parts[:, 0]] + [
        swap(hold(parts[:, rel], *middle), CT, rel) for rel in range(1, context_count)
    ]


def tree_info(parent_row):
    slot_count = parent_row.shape[0]
    slot_ids = jnp.arange(slot_count, dtype=jnp.int32)
    reach = (parent_row[:, None] == slot_ids[None, :]) | (slot_ids[:, None] == slot_ids[None, :])
    span = 1
    while span < slot_count:
        reach = jnp.any(reach[:, :, None] & reach[None, :, :], 1)
        span *= 2
    depths = jnp.sum(reach.astype(jnp.int32), 1) - 1
    return (reach, depths)


def rope_tables(positions, head_dim):
    half_dim = head_dim // 2
    frequency = ROPE_BASE ** (-2.0 * jnp.arange(half_dim, dtype=F32) / head_dim)
    angles = positions.astype(F32)[:, None] * frequency[None, :]
    cosine = jnp.concatenate([jnp.cos(angles), jnp.cos(angles)], -1)
    return (cosine, jnp.concatenate([-jnp.sin(angles), jnp.sin(angles)], -1))


def own_slots(chosen, order, first_expert, expert_dev, capacity):
    expert_ids = first_expert + jnp.arange(expert_dev, dtype=jnp.int32)
    hit = chosen[:, :, :, None] == expert_ids
    rank = jnp.sum(jnp.where(hit, order[:, :, :, None], 0), 2)
    routed = jnp.any(hit, 2)
    rank = jnp.where(routed, rank, 2**30).transpose(0, 2, 1)
    routed = routed.transpose(0, 2, 1)
    place = jnp.sum((rank[:, :, None, :] < rank[:, :, :, None]).astype(jnp.int32), -1)
    return jnp.where(routed & (place < capacity), place, -1)


def split_low(value):
    high = low(value)
    return [high, low(value - wide(high))]


def compiler_params():
    return pltpu.CompilerParams(vmem_limit_bytes=VMEM_BYTES)


def cost(microseconds):
    return pl.CostEstimate(
        flops=int(microseconds * 1e9), bytes_accessed=0, transcendentals=0
    )


def column_chunks(width):
    starts = list(range(0, width, CHUNK))
    return [slice(start, min(start + CHUNK, width)) for start in starts]


def choose_matrix(slots, pad):
    count, rows = slots.shape
    places = lax.broadcasted_iota(jnp.int32, (pad, rows), 0)
    parts = [
        jnp.where(slots[one : one + 1, :] == places, 1.0, 0.0) for one in range(count)
    ]
    return low(jnp.concatenate(parts, 0))


def choose_turned(slots, pad):
    count, rows = slots.shape
    expert = lax.broadcasted_iota(jnp.int32, (count, count * pad), 0)
    column = lax.broadcasted_iota(jnp.int32, (count, count * pad), 1)
    inside = (column >= expert * pad) & (column < (expert + 1) * pad)
    spread = dot(low(slots), low(jnp.where(inside, 1.0, 0.0)), 0, 0)
    place = jnp.sum(jnp.where(inside, column - expert * pad, 0), 0, keepdims=True)
    return low(jnp.where(spread == wide(place), 1.0, 0.0))


def load_block(step, blocks, buffer, sems):
    slots = buffer.shape[0]

    def copy(rel):
        return pltpu.make_async_copy(blocks[rel], buffer.at[rel % slots], sems.at[rel % slots])

    for rel in range(len(blocks)):

        @pl.when(step == rel)
        def _():
            if rel == 0:
                for ahead in range(min(slots, len(blocks)) - 1):
                    copy(ahead).start()
            if rel + slots - 1 < len(blocks):
                copy(rel + slots - 1).start()
            copy(rel).wait()


def split_refs(refs):
    parts = []
    for ref in refs:
        parts += [ref] if len(ref.shape) == 2 else [ref.at[one] for one in range(ref.shape[0])]
    return parts


def dispatch_kernel(pad, slots_ref, *refs):
    *blocks, out_ref, buffer, sems = refs
    blocks = split_refs(blocks)
    step = pl.program_id(0)
    load_block(step, blocks, buffer, sems)
    choose = choose_matrix(slots_ref[0], pad)
    count = slots_ref.shape[1]
    for cut in column_chunks(buffer.shape[2]):
        picked = low(dot(choose, buffer[lax.rem(step, buffer.shape[0]), :, cut]))
        for one in range(count):
            out_ref[one, 0, :, cut] = picked[one * pad : (one + 1) * pad]


def dispatch(slots, blocks, pad):
    group_count, expert_dev, rows = slots.shape
    width = blocks[0].shape[1]
    blocks = [array_of(block) for block in blocks if array_of(block) is block or block[1] == 0]
    return pl.pallas_call(
        functools.partial(dispatch_kernel, pad),
        grid=(group_count,),
        out_shape=jax.ShapeDtypeStruct((expert_dev, group_count, pad, width), BF16),
        in_specs=[pl.BlockSpec((1, expert_dev, rows), lambda i: (i, 0, 0))]
        + [pl.BlockSpec(memory_space=pl.ANY)] * len(blocks),
        out_specs=pl.BlockSpec((expert_dev, 1, pad, width), lambda i: (0, i, 0, 0)),
        scratch_shapes=[pltpu.VMEM((4, rows, width), BF16), pltpu.SemaphoreType.DMA((4,))],
        compiler_params=compiler_params(),
        cost_estimate=cost(12),
    )(slots, *blocks)


def combine_all(slots_ref, scratch, pad, outs, buffer, sems):
    count, pair_rows, width = scratch.shape
    group_count = len(outs)

    def copy(turn, source):
        return pltpu.make_async_copy(buffer.at[turn % 2], outs[source], sems.at[turn % 2])

    def body(turn, carry):
        source = lax.rem(turn + group_count // 2, group_count)
        choose = choose_turned(slots_ref[source], pad)
        start = pl.multiple_of(source * pad, pad)

        @pl.when(turn >= 2)
        def _():
            copy(turn, 0).wait()

        for cut in column_chunks(width):
            picked = scratch[:, pl.ds(start, pad), cut].reshape(count * pad, cut.stop - cut.start)
            buffer[turn % 2, :, cut] = low(dot(choose, picked))

        for one in range(group_count):

            @pl.when(source == one)
            def _():
                copy(turn, one).start()

        return carry

    lax.fori_loop(0, group_count, body, 0)
    for turn in range(group_count - 2, group_count):
        copy(turn, 0).wait()


def experts_kernel(
    group_count,
    pad,
    pieces,
    expert_count,
    first_ref,
    slots_ref,
    grads_ref,
    gate_ref,
    up_ref,
    down_ref,
    *refs,
):
    blocks = refs[:group_count]
    rows_out, act_out, back_out = refs[group_count : group_count + 3]
    outs = refs[group_count + 3 : 2 * group_count + 3]
    buffer, row_scratch, back_scratch, gate_scratch, sems, out_sems = refs[2 * group_count + 3 :]
    expert_dev, pair_rows, width = row_scratch.shape
    piece_rows = pair_rows // pieces
    hidden = gate_ref.shape[2]
    step = pl.program_id(0)

    def out_copy(one):
        return pltpu.make_async_copy(row_scratch.at[one], rows_out.at[one], out_sems.at[one])

    def pick(source, carry):
        load_block(source, blocks, buffer, sems)
        choose = choose_matrix(slots_ref[source], pad)
        start = pl.multiple_of(source * pad, pad)
        for cut in column_chunks(width):
            picked = low(dot(choose, buffer[lax.rem(source, buffer.shape[0]), :, cut]))
            for one in range(expert_dev):
                row_scratch[one, pl.ds(start, pad), cut] = picked[one * pad : (one + 1) * pad]
        gates = dot(choose, buffer[lax.rem(source, buffer.shape[0]), :, width:])
        gates = gates[:, :expert_count] + gates[:, expert_count:]
        column = lax.broadcasted_iota(jnp.int32, (pad, expert_count), 1)
        for one in range(expert_dev):
            own = column == first_ref[0] + one
            gate_scratch[one, pl.ds(start, pad), :] = jnp.sum(
                jnp.where(own, gates[one * pad : (one + 1) * pad], 0.0), -1, keepdims=True
            )
        return carry

    @pl.when(step == 0)
    def _():
        lax.fori_loop(0, group_count, pick, 0)

    one = step // pieces
    start = pl.multiple_of(lax.rem(step, pieces) * piece_rows, piece_rows)
    span = pl.ds(start, piece_rows)

    @pl.when(start == 0)
    def _():
        out_copy(one).start()

    rows = row_scratch[one, span, :]
    gate_proj = dot(rows, gate_ref[0])
    up_proj = dot(rows, up_ref[0])
    act_raw = dot(grads_ref[0], down_ref[0], 1, 1)
    gates = gate_scratch[one, span, :]
    sigmoid_gate = 1.0 / (1.0 + jnp.exp(-gate_proj))
    silu_gate = gate_proj * sigmoid_gate
    activated = wide(low(silu_gate * up_proj))
    dots = jnp.sum(activated * act_raw, -1, keepdims=True)
    act_grad = act_raw * gates
    gate_low = low(act_grad * up_proj * sigmoid_gate * (1.0 + gate_proj * (1.0 - sigmoid_gate)))
    up_low = low(act_grad * silu_gate)
    act_out[0] = low(activated * gates)
    back_out[0, :, :hidden] = gate_low
    back_out[0, :, hidden:] = up_low
    for cut in column_chunks(width):
        back_scratch[one, span, cut] = low(
            dot(gate_low, gate_ref[0, cut, :], 1, 1) + dot(up_low, up_ref[0, cut, :], 1, 1)
        )
    column = lax.broadcasted_iota(jnp.int32, (piece_rows, expert_count), 1)
    spread = jnp.where(column == first_ref[0] + one, dots, 0.0)
    back_scratch[one, span, width:] = jnp.concatenate(split_low(spread), 1)

    @pl.when(step == expert_dev * pieces - 1)
    def _():
        combine_all(slots_ref, back_scratch, pad, outs, buffer, sems)
        for one in range(expert_dev):
            out_copy(one).wait()


def experts(first, slots, blocks, grad_rows, w_gate, w_up, w_down, pad, expert_count):
    group_count, expert_dev, rows = slots.shape
    _, width, hidden = w_gate.shape
    pair_rows = group_count * pad
    pieces = max(1, pair_rows // 384)
    piece_rows = pair_rows // pieces
    full = blocks[0].shape[1]
    whole = pl.BlockSpec(slots.shape, lambda i: (0, 0, 0))
    into = pl.BlockSpec((1, width, hidden), lambda i: (i // pieces, 0, 0))
    onto = pl.BlockSpec((1, hidden, width), lambda i: (i // pieces, 0, 0))

    def piece(size):
        return pl.BlockSpec((1, piece_rows, size), lambda i: (i // pieces, lax.rem(i, pieces), 0))

    pairs = expert_dev * pair_rows
    return pl.pallas_call(
        functools.partial(experts_kernel, group_count, pad, pieces, expert_count),
        grid=(expert_dev * pieces,),
        out_shape=[
            jax.ShapeDtypeStruct((expert_dev, pair_rows, size), BF16)
            for size in (width, hidden, 2 * hidden)
        ]
        + [jax.ShapeDtypeStruct((rows, full), BF16)] * group_count,
        in_specs=[pl.BlockSpec(memory_space=pltpu.SMEM), whole, piece(width), into, into, onto]
        + [pl.BlockSpec(memory_space=pl.ANY)] * group_count,
        out_specs=[pl.BlockSpec(memory_space=pl.ANY), piece(hidden), piece(2 * hidden)]
        + [pl.BlockSpec(memory_space=pl.ANY)] * group_count,
        scratch_shapes=[
            pltpu.VMEM((4, rows, full), BF16),
            pltpu.VMEM((expert_dev, pair_rows, width), BF16),
            pltpu.VMEM((expert_dev, pair_rows, full), BF16),
            pltpu.VMEM((expert_dev, pair_rows, 1), F32),
            pltpu.SemaphoreType.DMA((4,)),
            pltpu.SemaphoreType.DMA((expert_dev,)),
        ],
        compiler_params=compiler_params(),
        cost_estimate=cost(100),
    )(first, slots, grad_rows, w_gate, w_up, w_down, *blocks)


def expert_out_kernel(pad, pieces, skip, slots_ref, act_ref, down_ref, *refs):
    outs, (scratch, buffer, sems) = split_refs(refs[skip:-3]), refs[-3:]
    expert_dev, pair_rows, width = scratch.shape
    piece_rows = pair_rows // pieces
    step = pl.program_id(0)
    start = pl.multiple_of(lax.rem(step, pieces) * piece_rows, piece_rows)
    for cut in column_chunks(width):
        scratch[step // pieces, pl.ds(start, piece_rows), cut] = low(
            dot(act_ref[0], down_ref[0, :, cut])
        )

    @pl.when(step == expert_dev * pieces - 1)
    def _():
        combine_all(slots_ref, scratch, pad, outs, buffer, sems)


def expert_out(slots, act, w_down, pad, near, *earlier):
    group_count, expert_dev, rows = slots.shape
    _, hidden, width = w_down.shape
    pair_rows = group_count * pad
    pieces = max(1, pair_rows // 384)
    pairs = expert_dev * pair_rows
    return pl.pallas_call(
        functools.partial(expert_out_kernel, pad, pieces, len(earlier)),
        grid=(expert_dev * pieces,),
        out_shape=[jax.ShapeDtypeStruct((rows, width), BF16)] * near
        + [jax.ShapeDtypeStruct((group_count - near, rows, width), BF16)],
        in_specs=[
            pl.BlockSpec(slots.shape, lambda i: (0, 0, 0)),
            pl.BlockSpec(
                (1, pair_rows // pieces, hidden), lambda i: (i // pieces, lax.rem(i, pieces), 0)
            ),
            pl.BlockSpec((1, hidden, width), lambda i: (i // pieces, 0, 0)),
        ]
        + [pl.BlockSpec(memory_space=pl.ANY)] * len(earlier),
        out_specs=[pl.BlockSpec(memory_space=pl.ANY)] * (near + 1),
        scratch_shapes=[
            pltpu.VMEM((expert_dev, pair_rows, width), BF16),
            pltpu.VMEM((2, rows, width), BF16),
            pltpu.SemaphoreType.DMA((2,)),
        ],
        compiler_params=compiler_params(),
        cost_estimate=cost(40),
    )(slots, act, w_down, *earlier)


def weight_grad_kernel(pieces, skip, left_ref, right_ref, *outs):
    outs = outs[skip:]
    inside = lax.rem(pl.program_id(0), pieces)
    size = outs[0].shape[2]
    tall = left_ref.shape[2] >= right_ref.shape[2]

    def add(out_ref, index, term):
        if pieces == 1:
            out_ref[index] = term
        else:

            @pl.when(inside == 0)
            def _():
                out_ref[index] = term

            @pl.when(inside > 0)
            def _():
                out_ref[index] += term

    if tall:
        for cut in column_chunks(left_ref.shape[2]):
            term = dot(left_ref[0, :, cut], right_ref[0], 0, 0)
            for one, out_ref in enumerate(outs):
                add(out_ref, (0, cut), term[:, one * size : (one + 1) * size])
    else:
        for cut in column_chunks(right_ref.shape[2]):
            add(outs[0], (0, slice(None), cut), dot(left_ref[0], right_ref[0, :, cut], 0, 0))


def weight_grad(left, right, count, *earlier):
    expert_dev, pair_rows, tall = left.shape
    size = right.shape[2] // count
    pieces = max(1, pair_rows // 384)

    def piece(width):
        return pl.BlockSpec(
            (1, pair_rows // pieces, width), lambda i: (i // pieces, lax.rem(i, pieces), 0)
        )

    return pl.pallas_call(
        functools.partial(weight_grad_kernel, pieces, len(earlier)),
        grid=(expert_dev * pieces,),
        out_shape=[jax.ShapeDtypeStruct((expert_dev, tall, size), F32)] * count,
        in_specs=[piece(tall), piece(right.shape[2])]
        + [pl.BlockSpec(memory_space=pl.ANY)] * len(earlier),
        out_specs=[pl.BlockSpec((1, tall, size), lambda i: (i // pieces, 0, 0))] * count,
        compiler_params=compiler_params(),
        cost_estimate=cost(80),
    )(left, right, *earlier)


def scatter_dot_kernel(index_ref, value_ref, *refs):
    blocks, out_ref = refs[:-1], refs[-1]
    depth = blocks[0].shape[0]
    for rel, block in enumerate(blocks):
        start = pl.multiple_of((index_ref[0] ^ rel) * depth, depth)
        part = dot(value_ref[...], block[...], 1, 1)
        out_ref[:, pl.ds(start, depth)] = part.astype(out_ref.dtype)


def scatter_dot(index, value, blocks, cut, kind):
    rows = value.shape[0]
    depth = blocks[0].shape[0]
    size = cut.stop - cut.start
    if depth % 128:
        whole = place_rows([plain(block)[:, cut] for block in blocks], index)
        return dot(value, whole, 1, 1).astype(kind)
    first = cut.start // size
    return pl.pallas_call(
        scatter_dot_kernel,
        grid=(1,),
        out_shape=jax.ShapeDtypeStruct((rows, depth * len(blocks)), kind),
        in_specs=[
            pl.BlockSpec(memory_space=pltpu.SMEM),
            pl.BlockSpec((rows, size), lambda i: (0, 0)),
        ]
        + [block_spec(block, size, first) for block in blocks],
        out_specs=pl.BlockSpec((rows, depth * len(blocks)), lambda i: (0, 0)),
        compiler_params=compiler_params(),
        cost_estimate=cost(12),
    )(index.reshape(1), value, *[array_of(block) for block in blocks])


def attend_kernel(score_scale, context_count, query_ref, bias_ref, *refs):
    blocks = refs[:context_count]
    out_ref, total_ref = refs[context_count:]
    head_dim = query_ref.shape[1]
    scores = jnp.concatenate(
        [dot(query_ref[...], block[:, :head_dim], 1, 1) for block in blocks], 1
    )
    scores = scores * score_scale + bias_ref[...]
    row_peak = jnp.max(scores, -1, keepdims=True)
    weights = jnp.exp(scores - row_peak)
    row_total = jnp.sum(weights, -1, keepdims=True)
    probabilities = low(weights / row_total)
    rows = query_ref.shape[0]
    attended = sum(
        dot(probabilities[:, rel * rows : (rel + 1) * rows], block[:, head_dim:])
        for rel, block in enumerate(blocks)
    )
    out_ref[...] = low(attended)
    total_ref[0] = row_peak + jnp.log(row_total)


def attend(queries, blocks, bias, head_dim):
    rows, head_width = queries.shape
    heads = head_width // head_dim
    one = pl.BlockSpec((rows, head_dim), lambda h: (0, h))
    two = pl.BlockSpec((rows, 2 * head_dim), lambda h: (0, h))
    return pl.pallas_call(
        functools.partial(attend_kernel, head_dim ** (-0.5), len(blocks)),
        grid=(heads,),
        out_shape=[
            jax.ShapeDtypeStruct((rows, head_width), BF16),
            jax.ShapeDtypeStruct((heads, rows, 1), F32),
        ],
        in_specs=[one, pl.BlockSpec(bias.shape, lambda h: (0, 0))] + [two] * len(blocks),
        out_specs=[one, pl.BlockSpec((1, rows, 1), lambda h: (h, 0, 0))],
        compiler_params=compiler_params(),
        cost_estimate=cost(12),
    )(queries, bias, *blocks)


def attend_back_kernel(score_scale, context_count, query_ref, grad_ref, total_ref, bias_ref, *refs):
    blocks = refs[:context_count]
    query_out, outs = refs[context_count], refs[context_count + 1 :]
    rows, head_dim = query_ref.shape
    query, grad = query_ref[...], grad_ref[...]
    scores = jnp.concatenate([dot(query, block[:, :head_dim], 1, 1) for block in blocks], 1)
    probabilities = jnp.exp(scores * score_scale + bias_ref[...] - total_ref[0])
    prob_grad = jnp.concatenate([dot(grad, block[:, head_dim:], 1, 1) for block in blocks], 1)
    score_grad = probabilities * (
        prob_grad - jnp.sum(probabilities * prob_grad, -1, keepdims=True)
    )
    score_low = low(score_grad * score_scale)
    prob_low = low(probabilities)
    query_grad = jnp.zeros((rows, head_dim), F32)
    for rel, (block, out) in enumerate(zip(blocks, outs)):
        cut = slice(rel * rows, (rel + 1) * rows)
        query_grad = query_grad + dot(score_low[:, cut], block[:, :head_dim])
        out[:, :head_dim] = low(dot(score_low[:, cut], query, 0, 0))
        out[:, head_dim:] = low(dot(prob_low[:, cut], grad, 0, 0))
    query_out[...] = query_grad


def attend_back(queries, grads, totals, blocks, bias, head_dim):
    rows, head_width = queries.shape
    heads = head_width // head_dim
    one = pl.BlockSpec((rows, head_dim), lambda h: (0, h))
    two = pl.BlockSpec((rows, 2 * head_dim), lambda h: (0, h))
    return pl.pallas_call(
        functools.partial(attend_back_kernel, head_dim ** (-0.5), len(blocks)),
        grid=(heads,),
        out_shape=[jax.ShapeDtypeStruct((rows, head_width), F32)]
        + [jax.ShapeDtypeStruct((rows, 2 * head_width), BF16)] * len(blocks),
        in_specs=[
            one,
            one,
            pl.BlockSpec((1, rows, 1), lambda h: (h, 0, 0)),
            pl.BlockSpec(bias.shape, lambda h: (0, 0)),
        ]
        + [two] * len(blocks),
        out_specs=[one] + [two] * len(blocks),
        compiler_params=compiler_params(),
        cost_estimate=cost(12),
    )(queries, grads, totals, bias, *blocks)


def row_norm(values):
    return lax.rsqrt(jnp.mean(values * values, -1, keepdims=True) + EPS)


def chunk(index_ref, rel, size):
    return pl.ds(pl.multiple_of((index_ref[0] ^ rel) * size, size), size)


def whole_spec(value):
    return pl.BlockSpec(value.shape, lambda i: (0,) * value.ndim)


def column_spec(value, size, first=0):
    return pl.BlockSpec((value.shape[0], size), lambda i: (0, first + i))


def project_kernel(group_count, heads, index_ref, hidden_ref, *refs):
    smalls, blocks = refs[:group_count], refs[group_count : 2 * group_count]
    attn_ref, out_ref, square_ref, scale_ref, moe_ref, gain_ref = refs[2 * group_count :]
    depth = blocks[0].shape[0]
    piece = gain_ref.shape[1] // (2 * heads * group_count)
    used = 2 * heads * piece

    @pl.when(pl.program_id(0) == 0)
    def _():
        scale = row_norm(wide(hidden_ref[...]))
        scale_ref[...] = scale
        gains = jnp.zeros(gain_ref.shape, F32)
        for rel, small in enumerate(smalls):
            cut = chunk(index_ref, rel, depth)
            columns = wide(small[...]).T
            attn_ref[:, cut] = low(wide(hidden_ref[:, cut]) * scale * columns[0:1, :])
            moe_ref[:, cut] = columns[0:2, :]
            row = lax.broadcasted_iota(jnp.int32, (depth, gain_ref.shape[1]), 0)
            column = lax.broadcasted_iota(jnp.int32, (depth, gain_ref.shape[1]), 1)
            inside = column - (index_ref[0] ^ rel) * piece - (row // piece) * piece * group_count
            place = (inside == lax.rem(row, piece)) & (row < used)
            gains = gains + dot(low(columns), low(jnp.where(place, 1.0, 0.0)))[2:3, :]
        gain_ref[...] = gains

    total = jnp.zeros(out_ref.shape, F32)
    for rel, block in enumerate(blocks):
        total = total + dot(attn_ref[:, chunk(index_ref, rel, depth)], block[...])
    out_ref[...] = total
    square_ref[0] = jnp.sum(total * total, -1, keepdims=True)


def project(index, hidden, blocks, tile, heads):
    rows, width = hidden.shape
    depth = blocks[0].shape[0]
    count = len(blocks)
    if depth % 128:
        packed = place_rows(blocks, index)
        hidden = wide(hidden)
        scale = row_norm(hidden)
        attn_in = low(hidden * scale * wide(packed[:, 3 * tile]))
        projected = dot(attn_in, packed[:, : 3 * tile])
        squares = jnp.sum((projected * projected).reshape(rows, 3, tile), -1).T
        norm_gains = wide(packed[:, 3 * tile : 3 * tile + 2]).T
        gains = wide(packed[:, 3 * tile + 2]).reshape(count, depth)[:, : 2 * tile // count]
        gains = gains.reshape(count, 2, heads, -1).transpose(1, 2, 0, 3).reshape(2, tile)
        return attn_in, projected, squares, scale, norm_gains, gains
    attn_in, projected, squares, scale, norm_gains, gains = pl.pallas_call(
        functools.partial(project_kernel, count, heads),
        grid=(3,),
        out_shape=[
            jax.ShapeDtypeStruct((rows, width), BF16),
            jax.ShapeDtypeStruct((rows, 3 * tile), F32),
            jax.ShapeDtypeStruct((3, rows, 1), F32),
            jax.ShapeDtypeStruct((rows, 1), F32),
            jax.ShapeDtypeStruct((2, width), F32),
            jax.ShapeDtypeStruct((1, 2 * tile), F32),
        ],
        in_specs=[pl.BlockSpec(memory_space=pltpu.SMEM), whole_spec(hidden)]
        + [pl.BlockSpec((depth, 128), lambda i: (0, 3 * tile // 128))] * count
        + [column_spec(blocks[0], tile)] * count,
        out_specs=[
            whole_spec(hidden),
            pl.BlockSpec((rows, tile), lambda i: (0, i)),
            pl.BlockSpec((1, rows, 1), lambda i: (i, 0, 0)),
            pl.BlockSpec((rows, 1), lambda i: (0, 0)),
            pl.BlockSpec((2, width), lambda i: (0, 0)),
            pl.BlockSpec((1, 2 * tile), lambda i: (0, 0)),
        ],
        compiler_params=compiler_params(),
        cost_estimate=cost(12),
    )(index.reshape(1), hidden, *blocks, *blocks)
    return attn_in, projected, squares[:, :, 0], scale, norm_gains, gains.reshape(2, tile)


def swapped(values):
    half = values.shape[1] // 2
    return jnp.concatenate([values[:, half:], values[:, :half]], 1)


def turn_kernel(query_ref, key_ref, value_ref, scale_ref, gain_ref, cos_ref, sin_ref, *outs):
    query_out, pair_out = outs
    size = query_ref.shape[1]
    for part, (source, out_ref) in enumerate([(query_ref, query_out), (key_ref, pair_out)]):
        hat = source[...] * scale_ref[part] * gain_ref[part : part + 1, :]
        out_ref[:, :size] = low(hat * cos_ref[...] + swapped(hat) * sin_ref[...])
    pair_out[:, size:] = low(value_ref[...])


def turn_heads(projected, scales, gains, cosine, sine, heads):
    rows, size = cosine.shape
    return pl.pallas_call(
        turn_kernel,
        grid=(heads,),
        out_shape=[
            jax.ShapeDtypeStruct((rows, heads * size), BF16),
            jax.ShapeDtypeStruct((rows, 2 * heads * size), BF16),
        ],
        in_specs=[column_spec(projected, size, part * heads) for part in range(3)]
        + [whole_spec(scales), column_spec(gains, size), whole_spec(cosine), whole_spec(sine)],
        out_specs=[
            pl.BlockSpec((rows, size), lambda i: (0, i)),
            pl.BlockSpec((rows, 2 * size), lambda i: (0, i)),
        ],
        compiler_params=compiler_params(),
        cost_estimate=cost(6),
    )(projected, projected, projected, scales, gains, cosine, sine)


def turn_back_kernel(part_count, *refs):
    query_grad, parts = refs[0], refs[1 : 1 + part_count]
    query_ref, key_ref, scale_ref, gain_ref, cos_ref, sin_ref = refs[1 + part_count : 7 + part_count]
    query_out, key_out, value_out, inner_out, gain_out = refs[7 + part_count :]
    size = query_ref.shape[1]
    total = sum(wide(part[...]) for part in parts)
    value_out[...] = low(total[:, size:])
    pairs = [(query_grad[...], query_ref, query_out), (total[:, :size], key_ref, key_out)]
    for part, (grad, source, out_ref) in enumerate(pairs):
        hat = source[...] * scale_ref[part]
        norm_grad = grad * cos_ref[...] - swapped(grad) * sin_ref[...]
        gain_out[part : part + 1, :] = jnp.sum(norm_grad * hat, 0, keepdims=True)
        hat_grad = norm_grad * gain_ref[part : part + 1, :]
        out_ref[...] = hat_grad
        inner = jnp.sum(hat_grad * hat, -1, keepdims=True)

        @pl.when(pl.program_id(0) == 0)
        def _():
            inner_out[part] = inner

        @pl.when(pl.program_id(0) > 0)
        def _():
            inner_out[part] += inner


def turn_back(query_grad, parts, projected, scales, gains, cosine, sine, heads):
    rows, size = cosine.shape
    one = pl.BlockSpec((rows, size), lambda i: (0, i))
    two = pl.BlockSpec((rows, 2 * size), lambda i: (0, i))
    return pl.pallas_call(
        functools.partial(turn_back_kernel, len(parts)),
        grid=(heads,),
        out_shape=[jax.ShapeDtypeStruct((rows, heads * size), kind) for kind in (F32, F32, BF16)]
        + [
            jax.ShapeDtypeStruct((2, rows, 1), F32),
            jax.ShapeDtypeStruct((2, heads * size), F32),
        ],
        in_specs=[one]
        + [two] * len(parts)
        + [column_spec(projected, size, part * heads) for part in range(2)]
        + [whole_spec(scales), column_spec(gains, size), whole_spec(cosine), whole_spec(sine)],
        out_specs=[
            one,
            one,
            one,
            pl.BlockSpec((2, rows, 1), lambda i: (0, 0, 0)),
            pl.BlockSpec((2, size), lambda i: (0, i)),
        ],
        compiler_params=compiler_params(),
        cost_estimate=cost(8),
    )(query_grad, *parts, projected, projected, scales, gains, cosine, sine)


def input_grad_kernel(*refs):
    index_ref, query_grad, key_grad, value_low, projected, scale_ref, inner_ref = refs[:7]
    blocks, (low_ref, part_ref) = refs[7:-2], refs[-2:]
    size = query_grad.shape[1]
    depth = blocks[0].shape[0]
    for part, grad in enumerate([query_grad, key_grad]):
        cut = slice(part * size, (part + 1) * size)
        hat = projected[:, cut] * scale_ref[part]
        low_ref[:, cut] = low(scale_ref[part] * (grad[...] - hat * inner_ref[part]))
    low_ref[:, 2 * size :] = value_low[...]
    for rel, block in enumerate(blocks):
        part_ref[:, chunk(index_ref, rel, depth)] = low(dot(low_ref[...], block[...], 1, 1))


def input_grad(index, query_grad, key_grad, value_low, projected, scales, inner, blocks):
    rows, size = query_grad.shape
    depth = blocks[0].shape[0]
    if depth % 128:
        parts = []
        for part, grad in enumerate([query_grad, key_grad]):
            hat = projected[:, part * size : (part + 1) * size] * scales[part]
            parts.append(low(scales[part] * (grad - hat * inner[part])))
        qkv_low = jnp.concatenate(parts + [value_low], 1)
        return qkv_low, low(dot(qkv_low, place_rows(blocks, index)[:, : 3 * size], 1, 1))
    weights = pl.BlockSpec((depth, 3 * size), lambda i: (0, 0))
    values = [query_grad, key_grad, value_low, projected, scales, inner]
    return pl.pallas_call(
        input_grad_kernel,
        grid=(1,),
        out_shape=[
            jax.ShapeDtypeStruct((rows, 3 * size), BF16),
            jax.ShapeDtypeStruct((rows, depth * len(blocks)), BF16),
        ],
        in_specs=[pl.BlockSpec(memory_space=pltpu.SMEM)]
        + [whole_spec(value) for value in values]
        + [weights] * len(blocks),
        out_specs=[
            pl.BlockSpec((rows, 3 * size), lambda i: (0, 0)),
            pl.BlockSpec((rows, depth * len(blocks)), lambda i: (0, 0)),
        ],
        compiler_params=compiler_params(),
        cost_estimate=cost(12),
    )(index.reshape(1), *values, *blocks)


def route_kernel(tensor_count, expert_count, index_ref, tensor_ref, gain_ref, *refs):
    parts, routers = refs[:tensor_count], refs[tensor_count:-4]
    sent_ref, probs_ref, residual_ref, scale_ref = refs[-4:]
    quarter = parts[0].shape[1]
    rows, width = residual_ref.shape
    depth = routers[0].shape[0]
    for rel, part in enumerate(parts):
        residual_ref[:, chunk(tensor_ref, rel, quarter)] = part[...]
    residual = wide(residual_ref[...])
    scale = row_norm(residual)
    scale_ref[...] = scale
    sent_ref[:, :width] = low(residual * scale * gain_ref[...])
    logits = jnp.zeros((rows, routers[0].shape[1]), F32)
    for rel, router in enumerate(routers):
        logits = logits + dot(sent_ref[:, chunk(index_ref, rel, depth)], router[...])
    logits = logits[:, :expert_count]
    exponent = jnp.exp(logits - jnp.max(logits, -1, keepdims=True))
    probs = exponent / jnp.sum(exponent, -1, keepdims=True)
    probs_ref[...] = probs
    sent_ref[:, width:] = jnp.concatenate(split_low(probs), 1)


def route(index, tensor_index, gain, parts, blocks, cut, expert_count):
    rows, quarter = parts[0].shape
    width = quarter * len(parts)
    depth = blocks[0].shape[0]
    if depth % 128:
        residual = jnp.concatenate(in_order(parts, tensor_index), 1)
        scale = row_norm(wide(residual))
        moe_in = low(wide(residual) * scale * gain)
        logits = dot(moe_in, place_rows([plain(block)[:, cut] for block in blocks], index))
        logits = logits[:, :expert_count]
        exponent = jnp.exp(logits - jnp.max(logits, -1, keepdims=True))
        probs = exponent / jnp.sum(exponent, -1, keepdims=True)
        return jnp.concatenate([moe_in] + split_low(probs), 1), probs, residual, scale
    size = cut.stop - cut.start
    shapes = [(width + 2 * expert_count, BF16), (expert_count, F32), (width, BF16), (1, F32)]
    scalar = pl.BlockSpec(memory_space=pltpu.SMEM)
    return pl.pallas_call(
        functools.partial(route_kernel, len(parts), expert_count),
        grid=(1,),
        out_shape=[jax.ShapeDtypeStruct((rows, one), kind) for one, kind in shapes],
        in_specs=[scalar, scalar, whole_spec(gain)]
        + [whole_spec(part) for part in parts]
        + [block_spec(block, size, cut.start // size) for block in blocks],
        out_specs=[pl.BlockSpec((rows, one), lambda i: (0, 0)) for one, _ in shapes],
        compiler_params=compiler_params(),
        cost_estimate=cost(8),
    )(index.reshape(1), tensor_index.reshape(1), gain, *parts, *[array_of(b) for b in blocks])


def residual_kernel(tensor_count, group_count, index_ref, tensor_ref, *refs):
    gain_ref, logit_ref, residual_ref, scale_ref, grad_ref = refs[:5]
    parts, refs = refs[5 : 5 + tensor_count], refs[5 + tensor_count :]
    routers, blocks = refs[:group_count], refs[group_count : 2 * group_count]
    low_ref, share_ref, gain_out, heads_ref, scratch = refs[2 * group_count :]
    quarter = parts[0].shape[1]
    depth = blocks[0].shape[0]
    for rel, part in enumerate(parts):
        scratch[:, chunk(tensor_ref, rel, quarter)] = wide(part[...])
    for rel, router in enumerate(routers):
        scratch[:, chunk(index_ref, rel, depth)] += dot(logit_ref[...], router[...], 1, 1)
    normed = wide(residual_ref[...]) * scale_ref[...]
    gain_out[...] = jnp.sum(scratch[...] * normed, 0, keepdims=True)
    normed_grad = scratch[...] * gain_ref[...]
    mean = jnp.mean(normed_grad * normed, -1, keepdims=True)
    scratch[...] = wide(grad_ref[...]) + scale_ref[...] * (normed_grad - normed * mean)
    low_ref[...] = low(scratch[...])
    share_ref[...] = scratch[:, chunk(tensor_ref, 0, quarter)]
    total = jnp.zeros(heads_ref.shape, F32)
    for rel, block in enumerate(blocks):
        total = total + dot(low_ref[:, chunk(index_ref, rel, depth)], block[...])
    heads_ref[...] = low(total)


def residual_back(index, tensor_index, gain, logit, residual, scale, grad, parts, blocks, heads, cut):
    rows, quarter = parts[0].shape
    width = quarter * len(parts)
    depth = blocks[0].shape[0]
    if depth % 128:
        whole = place_rows([plain(block) for block in blocks], index)
        moe_in_grad = wide(jnp.concatenate(in_order(parts, tensor_index), 1))
        moe_in_grad = moe_in_grad + dot(logit, whole[:, cut], 1, 1)
        normed = wide(residual) * scale
        gain_grad = jnp.sum(moe_in_grad * normed, 0, keepdims=True)
        normed_grad = moe_in_grad * gain
        mean = jnp.mean(normed_grad * normed, -1, keepdims=True)
        total = wide(grad) + scale * (normed_grad - normed * mean)
        share = lax.dynamic_slice_in_dim(total, tensor_index * quarter, quarter, 1)
        return low(total), share, gain_grad, low(dot(low(total), whole[:, :heads]))
    size = cut.stop - cut.start
    shapes = [(rows, width, BF16), (rows, quarter, F32), (1, width, F32), (rows, heads, BF16)]
    scalar = pl.BlockSpec(memory_space=pltpu.SMEM)
    values = [gain, logit, residual, scale, grad] + parts
    arrays = [array_of(block) for block in blocks]
    return pl.pallas_call(
        functools.partial(residual_kernel, len(parts), len(blocks)),
        grid=(1,),
        out_shape=[jax.ShapeDtypeStruct((one, two), kind) for one, two, kind in shapes],
        in_specs=[scalar, scalar]
        + [whole_spec(value) for value in values]
        + [block_spec(block, size, cut.start // size) for block in blocks]
        + [block_spec(block, heads, 0) for block in blocks],
        out_specs=[pl.BlockSpec((one, two), lambda i: (0, 0)) for one, two, _ in shapes],
        scratch_shapes=[pltpu.VMEM((rows, width), F32)],
        compiler_params=compiler_params(),
        cost_estimate=cost(12),
    )(index.reshape(1), tensor_index.reshape(1), *values, *arrays, *arrays)


def late_dot_kernel(part_count, index_ref, *refs):
    traded, late = refs[:part_count], refs[part_count : 2 * part_count]
    blocks, (out_ref, router_ref) = refs[2 * part_count : -2], refs[-2:]
    tall, size = out_ref.shape
    total, router = jnp.zeros(out_ref.shape, F32), jnp.zeros(router_ref.shape, F32)
    for rel, block in enumerate(blocks):
        right = late[rel % part_count][rel // part_count]
        left = traded[rel % part_count][rel // part_count, :, :tall]
        total = total + dot(left, right[:, :size], 0, 0)
        router = router + dot(block[...], right[:, size:], 0, 0)
    out_ref[...] = total
    router_ref[...] = router


def late_dots(index, traded, late, blocks, tall, size):
    rows = blocks[0].shape[0]
    experts = late[0].shape[2] - size
    if size % 128:
        shard_count = traded[0].shape[0]
        left = jnp.concatenate([part[one] for one in range(shard_count) for part in traded])
        right = jnp.concatenate([part[one] for one in range(shard_count) for part in late])
        inputs = [lax.dynamic_slice_in_dim(block, index * size, size, 1) for block in blocks]
        out_grad = dot(left[:, :tall], right[:, :size], 0, 0)
        return out_grad, dot(jnp.concatenate(inputs), right[:, size:], 0, 0)
    return pl.pallas_call(
        functools.partial(late_dot_kernel, len(traded)),
        grid_spec=pltpu.PrefetchScalarGridSpec(
            num_scalar_prefetch=1,
            grid=(1,),
            in_specs=[pl.BlockSpec(one.shape, lambda i, s: (0, 0, 0)) for one in traded + late]
            + [pl.BlockSpec((rows, size), lambda i, s: (0, s[0]))] * len(blocks),
            out_specs=[
                pl.BlockSpec((tall, size), lambda i, s: (0, 0)),
                pl.BlockSpec((size, experts), lambda i, s: (0, 0)),
            ],
        ),
        out_shape=[
            jax.ShapeDtypeStruct((tall, size), F32),
            jax.ShapeDtypeStruct((size, experts), F32),
        ],
        compiler_params=compiler_params(),
        cost_estimate=cost(6),
    )(index.reshape(1), *traded, *late, *blocks)


def qkv_dot_kernel(part_count, first, *refs):
    traded, grads, outs = refs[:part_count], refs[part_count:-3], refs[-3:]
    size = outs[0].shape[1]
    for one, out_ref in enumerate(outs):
        total = jnp.zeros(out_ref.shape, F32)
        for rel, grad in enumerate(grads):
            left = traded[rel % part_count][rel // part_count, :, first:]
            total = total + dot(left, grad[:, one * size : (one + 1) * size], 0, 0)
        out_ref[...] = total


def qkv_dots(traded, grads, first, size):
    tall = traded[0].shape[2] - first
    if tall % 128:
        shard_count = traded[0].shape[0]
        left = jnp.concatenate([part[one] for one in range(shard_count) for part in traded])
        total = dot(left[:, first:], jnp.concatenate(grads), 0, 0)
        return [total[:, one * size : (one + 1) * size] for one in range(3)]
    return pl.pallas_call(
        functools.partial(qkv_dot_kernel, len(traded), first),
        grid=(1,),
        out_shape=[jax.ShapeDtypeStruct((tall, size), F32)] * 3,
        in_specs=[whole_spec(one) for one in traded + grads],
        out_specs=[pl.BlockSpec((tall, size), lambda i: (0, 0))] * 3,
        compiler_params=compiler_params(),
        cost_estimate=cost(8),
    )(*traded, *grads)


def per_device(
    tokens,
    parents,
    routes,
    pair_order,
    norm_attn,
    w_query,
    w_key,
    w_value,
    q_gain,
    k_gain,
    w_out,
    norm_moe,
    w_router,
    w_gate,
    w_up,
    w_down,
    out_grad,
):
    shard_index, context_index, tensor_index = (lax.axis_index(a) for a in (SH, CT, TS))
    context_count, tensor_count = lax.axis_size(CT), lax.axis_size(TS)
    group_count = lax.axis_size(SH) * context_count
    group = shard_index * context_count + context_index
    seg_dev, seg_len, quarter = tokens.shape[1:]
    rows = seg_dev * seg_len
    model_width = quarter * tensor_count
    slice_width = norm_attn.shape[0]
    top_count = routes.shape[3]
    expert_count = w_router.shape[1]
    expert_dev = w_gate.shape[0]
    local_heads, head_dim = q_gain.shape[0], q_gain.shape[1] * group_count
    head_width = local_heads * head_dim
    capacity = tensor_count * (
        (5 * rows * top_count + 4 * expert_count * tensor_count - 1)
        // (4 * expert_count * tensor_count)
    )
    score_scale = head_dim ** (-0.5)

    out_cut = slice(0, head_width)
    router_pad = -expert_count % 128
    router_cut = slice(head_width, head_width + expert_count + router_pad)
    gain_size = q_gain.size
    gain_values = jnp.concatenate([q_gain.reshape(-1), k_gain.reshape(-1)])
    gain_values = jnp.pad(gain_values, (0, slice_width - 2 * gain_size))
    base = 64
    order = jnp.arange(seg_dev, dtype=jnp.int32)[:, None] * (seg_len * top_count) + pair_order[0]
    order = order.reshape(rows, top_count)
    codes = jnp.concatenate([routes.reshape(rows, top_count), order // base, order % base], 1)
    codes = low(codes).reshape(slice_width, -1)
    columns = jnp.stack([norm_attn, norm_moe, gain_values], 1)
    columns = jnp.concatenate([columns, codes], 1)
    columns = jnp.pad(columns, ((0, 0), (0, 128 - columns.shape[1])))
    packed = jnp.concatenate([w_query, w_key, w_value, columns], 1)
    token_parts = around(hold(tokens.reshape(rows, quarter), packed), TS)
    grad_parts = double(hold(out_grad.reshape(1, rows, quarter), *token_parts[1:]), TS)
    qkv_blocks = gather_groups(packed, *token_parts[1:])
    hidden_in = jnp.concatenate(in_order(token_parts, tensor_index), 1)
    grad_output = jnp.concatenate(in_order(grad_parts, tensor_index), 1)

    first_code = 3 * head_width + 3
    codes = [block[:, first_code : first_code + codes.shape[1]] for block in qkv_blocks]
    codes = jnp.stack(codes).reshape(group_count, rows, 3, top_count).astype(jnp.int32)
    slots = own_slots(
        codes[:, :, 0],
        codes[:, :, 1] * base + codes[:, :, 2],
        group * expert_dev,
        expert_dev,
        capacity,
    )
    pad = -(-capacity // 16) * 16

    reachable, depths = tree_info(parents[0])
    first_slot = context_index * seg_dev
    local_depth = lax.dynamic_slice_in_dim(depths, first_slot, seg_dev, 0)
    offsets = jnp.arange(seg_len, dtype=jnp.int32)
    positions = (local_depth[:, None] * seg_len + offsets[None, :]).reshape(rows)
    cosine, sine = rope_tables(positions, head_dim)
    reach_local = lax.dynamic_slice_in_dim(reachable, first_slot, seg_dev, 0)
    masks = []
    for rel in range(context_count):
        other_slot = (context_index ^ rel) * seg_dev
        seen = lax.dynamic_slice_in_dim(reach_local, other_slot, seg_dev, 1)
        seen = seen[:, None, :, None]
        if rel == 0:
            same = jnp.eye(seg_dev, dtype=bool)[:, None, :, None]
            seen = seen & (~same | (offsets[None, :] <= offsets[:, None])[None, :, None, :])
        masks.append(jnp.broadcast_to(seen, (seg_dev, seg_len, seg_dev, seg_len)).reshape(rows, rows))
    bias = jnp.where(jnp.concatenate(masks, 1), 0.0, NEG_FILL)

    attn_in, projected, squares, scale_attn, norm_gains, gains = project(
        group, hidden_in, qkv_blocks, head_width, local_heads
    )
    gain_attn, gain_moe = norm_gains[0], norm_gains[1:]
    out_blocks = jnp.concatenate([w_out.T, jnp.pad(w_router, ((0, 0), (0, router_pad)))], 1)
    out_blocks = hold(out_blocks, qkv_blocks[context_count - 1])
    out_blocks = stack_far(gather_context(out_blocks, projected))
    squares = sum(around(squares[:2], TS))
    scales = lax.rsqrt(squares / model_width + EPS)[:, :, None]
    scales = hold(scales, grad_parts)
    query_rot, key_value = turn_heads(projected, scales, gains, cosine, sine, local_heads)
    key_value = gather_context(hold(key_value, *out_blocks[1:context_count]))
    query_rot = hold(query_rot, slots)
    attended_low, log_total = attend(query_rot, key_value, bias, head_dim)

    def tensor_parts(value):
        return [
            lax.dynamic_slice_in_dim(value, (tensor_index ^ rel) * quarter, quarter, 1)
            for rel in range(tensor_count)
        ]

    def tensor_sum(parts):
        total = wide(parts[0])
        for rel in range(1, tensor_count):
            total = total + wide(swap(low(parts[rel]), TS, rel))
        return total

    attn_part = scatter_dot(group, attended_low, out_blocks, out_cut, F32)
    attn_share = tensor_sum(tensor_parts(attn_part))
    residual_share = wide(tokens.reshape(rows, quarter)) + attn_share
    grad_blocks = gather_context(hold(grad_output, *key_value[1:]), residual_share)
    parts = around(low(residual_share), TS)
    parts[-1] = hold(parts[-1], grad_blocks[-1])
    sent, router_probs, residual, scale_moe = route(
        group, tensor_index, gain_moe, parts, out_blocks, router_cut, expert_count
    )
    moe_in = sent[:, :model_width]
    grad_blocks = stack_far(grad_blocks[:-1] + [hold(grad_blocks[-1], sent)])
    grad_rows = dispatch(slots, grad_blocks, pad)
    blocks = gather_groups(sent, grad_rows)
    grad_rows = grad_rows.reshape(expert_dev, group_count * pad, model_width)

    def slices(value):
        return [
            lax.dynamic_slice_in_dim(value, (group ^ rel) * slice_width, slice_width, 1)
            for rel in range(group_count)
        ]

    late = hold(jnp.concatenate([attended_low, attn_in], 1), blocks[1])
    traded = [jnp.concatenate([late[:, :head_width], one], 1) for one in slices(late[:, head_width:])]
    traded = trade_start(jnp.stack(traded), blocks[-1])
    first = (group * expert_dev).reshape(1)
    pair_rows, act_gated, pair_back, *row_parts = experts(
        first,
        slots,
        blocks,
        grad_rows,
        w_gate,
        w_up,
        w_down,
        pad,
        expert_count,
    )
    row_far = joint(row_parts[context_count:], *traded[1:])
    row_own = core_sum(row_far, row_parts[:context_count])
    row_came = context_start(row_own)
    *mixed_near, mixed_far = expert_out(
        slots, act_gated, w_down, pad, context_count, *[block[1] for block in row_own[1:]]
    )
    row_total = context_end(row_own, row_came, mixed_near[0])
    (down_grad,) = weight_grad(act_gated, grad_rows, 1, row_total)
    mixed_far = swap(mixed_far, SH, 1)
    (down_grad,) = weight_grad(act_gated, grad_rows, 1, row_total)

    row_low = low(row_total)
    parts = [
        jnp.concatenate([part, row_low[:, model_width:]], 1)
        for part in tensor_parts(row_low[:, :model_width])
    ]
    parts = [parts[0]] + [swap(parts[rel], TS, rel) for rel in range(1, tensor_count)]
    parts[-1] = hold(parts[-1], down_grad, mixed_far)
    row_share = sum(wide(part[:, :quarter]) for part in parts)
    gate_w_grad, up_w_grad = weight_grad(pair_rows, pair_back, 2, row_share)
    prob_grads = sum(wide(part[:, quarter:]) for part in in_order(parts, tensor_index))
    prob_grads = prob_grads[:, :expert_count] + prob_grads[:, expert_count:]
    logit_low = low(
        router_probs * (prob_grads - jnp.sum(prob_grads * router_probs, -1, keepdims=True))
    )
    mixed_far = hold(mixed_far, row_share)
    mixed_own = [(block, mixed_far[one]) for one, block in enumerate(mixed_near)]
    mixed_came = context_start(mixed_own)
    parts = around(low(row_share), TS)
    parts[-1] = hold(parts[-1], gate_w_grad, *mixed_came)
    logit_wide = jnp.pad(logit_low, ((0, 0), (0, router_pad)))
    residual_low, residual_share_grad, gain_moe_grad, grad_heads = residual_back(
        group,
        tensor_index,
        gain_moe,
        logit_wide,
        residual,
        scale_moe,
        grad_output,
        parts,
        out_blocks,
        head_width,
        router_cut,
    )
    mixed_total = context_end(mixed_own, mixed_came, gate_w_grad)
    query_grad, *key_value_grad = attend_back(
        query_rot, grad_heads, log_total, key_value, bias, head_dim
    )
    key_value_grad[-1] = hold(key_value_grad[-1], mixed_total)
    traded_late = [jnp.concatenate([one, logit_low], 1) for one in slices(residual_low)]
    key_value_grad = [(block,) for block in key_value_grad]
    key_value_grad = context_end(key_value_grad, context_start(key_value_grad))
    traded_late = trade_start(jnp.stack(traded_late), key_value_grad)
    key_value_grad = [key_value_grad]
    query_hat_grad, key_hat_grad, value_low, inner, gain_grads = turn_back(
        query_grad, key_value_grad, projected, scales, gains, cosine, sine, local_heads
    )
    inner = butterfly(inner[:, :, 0], TS)[:, :, None] / model_width
    inner = hold(inner, *traded_late[1:])
    qkv_low, attn_part = input_grad(
        group, query_hat_grad, key_hat_grad, value_low, projected, scales, inner, qkv_blocks
    )
    traded_late[0] = hold(traded_late[0], qkv_low)
    out_w_grad, router_grad = late_dots(
        group, traded, traded_late, blocks, head_width, slice_width
    )
    qkv_grads = gather_groups(qkv_low)
    attn_share = tensor_sum(tensor_parts(attn_part))
    attn_share = hold(attn_share, *qkv_grads[1:context_count])
    hidden_share = wide(tokens.reshape(rows, quarter))
    normed_share = hidden_share * scale_attn
    normed_in_grad = attn_share * lax.dynamic_slice_in_dim(gain_attn, tensor_index * quarter, quarter)
    inner = jnp.sum(normed_in_grad * normed_share, -1)
    ends = jnp.zeros((rows + model_width,), F32)
    ends = lax.dynamic_update_slice_in_dim(
        ends, jnp.sum(attn_share * normed_share, 0), rows + tensor_index * quarter, 0
    )
    ends = butterfly(lax.dynamic_update_slice_in_dim(ends, inner, 0, 0), TS)
    inner = ends[:rows, None] / model_width
    gain_attn_grad = ends[rows:]
    mixed_share = tensor_sum(tensor_parts(hold(mixed_total, attn_share)))
    mixed_out = low(residual_share + mixed_share).reshape(tokens.shape)
    traded[0] = hold(traded[0], out_w_grad, mixed_share)
    qkv_w_grads = qkv_dots(traded, qkv_grads, head_width, head_width)
    tokens_grad = residual_share_grad + scale_attn * (normed_in_grad - normed_share * inner)

    gain_grads = gain_grads.reshape(2, local_heads, group_count, -1)
    gain_grads = gain_grads.transpose(2, 0, 1, 3).reshape(group_count, 2 * gain_size)
    vectors = jnp.concatenate(
        [
            gain_attn_grad.reshape(group_count, slice_width),
            gain_moe_grad.reshape(group_count, slice_width),
            gain_grads,
        ],
        1,
    )
    vectors = jnp.concatenate(
        [
            lax.dynamic_slice_in_dim(vectors, group ^ rel, 1, 0)[:, None]
            for rel in range(group_count)
        ]
    )
    vectors = core_sum([vectors[context_count:]], [vectors[:context_count]])
    vectors = add_up(vectors[0])
    vectors = vectors[0] + sum(swap(vectors[rel], CT, rel) for rel in range(1, context_count))
    vectors = vectors[0]
    gain_grads = vectors[2 * slice_width :].reshape((2,) + q_gain.shape)
    return (
        mixed_out,
        tokens_grad.reshape(tokens.shape),
        vectors[:slice_width],
        *qkv_w_grads,
        gain_grads[0],
        gain_grads[1],
        out_w_grad,
        vectors[slice_width : 2 * slice_width],
        router_grad,
        gate_w_grad,
        up_w_grad,
        down_grad,
    )


def solution(mesh):
    both = (SH, CT)
    rows = P(SH, CT, None, TS)
    pairs = P(SH, CT, None, None)
    vector, matrix, turned = P(both), P(both, TS), P(TS, both)
    up, down = P(both, None, TS), P(both, TS, None)
    return jax.shard_map(
        per_device,
        mesh=mesh,
        in_specs=(
            rows,
            P(SH, None),
            pairs,
            P(SH, CT, None),
            vector,
            matrix,
            matrix,
            matrix,
            turned,
            turned,
            turned,
            vector,
            P(both, None),
            up,
            up,
            down,
            rows,
        ),
        out_specs=(
            rows,
            rows,
            vector,
            matrix,
            matrix,
            matrix,
            turned,
            turned,
            turned,
            vector,
            P(both, None),
            up,
            up,
            down,
        ),
        check_vma=False,
    )
```

```python
import functools

import jax
import jax.numpy as jnp
from jax import lax
from jax.experimental import pallas as pl
from jax.experimental.pallas import tpu as pltpu
from jax.sharding import PartitionSpec as P

EPS = 1e-05
ROPE_BASE = 10000.0
NEG_FILL = -1e30
SH, CT, TS = "shard", "context", "tensor"
F32, BF16 = jnp.float32, jnp.bfloat16
CHUNK = 512
VMEM_BYTES = 58 * 2**20


def swap(value, axis, rel):
    count = lax.axis_size(axis)
    return lax.ppermute(value, axis, [(i, i ^ rel) for i in range(count)])


def around(value, axis):
    return [value] + [swap(value, axis, rel) for rel in range(1, lax.axis_size(axis))]


def gather_context(value, *middle):
    half = value.shape[0] // 2
    if lax.axis_size(CT) != 4 or half % 16:
        return around(value, CT)
    first, second = hold(swap(value, CT, 1), *middle), hold(swap(value, CT, 2), *middle)
    third = [swap(first[:half], CT, 2), swap(second[half:], CT, 1)]
    return [value, first, second, jnp.concatenate(third)]


def gather_groups(value, *middle):
    blocks = gather_context(value, *middle)
    for rel in range(1, lax.axis_size(SH)):
        blocks = blocks + [swap(block, SH, rel) for block in blocks[: lax.axis_size(CT)]]
    return blocks


def stack_far(blocks):
    far = [swap(jnp.stack(blocks), SH, rel) for rel in range(1, lax.axis_size(SH))]
    return blocks + [(one, place) for one in far for place in range(len(blocks))]


def plain(block):
    return block[0][block[1]] if isinstance(block, tuple) else block


def array_of(block):
    return block[0] if isinstance(block, tuple) else block


def block_spec(block, size, column):
    if isinstance(block, tuple):
        array, place = block
        return pl.BlockSpec((None, array.shape[1], size), lambda i: (place, 0, column))
    return pl.BlockSpec((block.shape[0], size), lambda i: (0, column))


def butterfly(value, axis):
    rel = 1
    while rel < lax.axis_size(axis):
        value = value + swap(value, axis, rel)
        rel *= 2
    return value


def double(value, axis):
    rel = 1
    while rel < lax.axis_size(axis):
        value = jnp.concatenate([value, swap(value, axis, rel)])
        rel *= 2
    return value


def in_order(blocks, index):
    ordered = []
    for place in range(len(blocks)):
        picked = blocks[place]
        for mine in range(1, len(blocks)):
            picked = jnp.where(index == mine, blocks[place ^ mine], picked)
        ordered.append(picked)
    return ordered


def place_rows(blocks, index):
    rows = blocks[0].shape[0]
    whole = jnp.zeros((rows * len(blocks),) + blocks[0].shape[1:], blocks[0].dtype)
    for rel, block in enumerate(blocks):
        whole = lax.dynamic_update_slice_in_dim(whole, block, (index ^ rel) * rows, 0)
    return whole


def low(value):
    return value.astype(BF16)


def wide(value):
    return value.astype(F32)


def hold_kernel(*refs):
    pass


def hold(value, *others):
    if not others:
        return value
    anywhere = pl.BlockSpec(memory_space=pl.ANY)
    return pl.pallas_call(
        hold_kernel,
        out_shape=jax.ShapeDtypeStruct(value.shape, value.dtype),
        in_specs=[anywhere] * (1 + len(others)),
        out_specs=anywhere,
        input_output_aliases={0: 0},
        cost_estimate=pl.CostEstimate(flops=0, bytes_accessed=0, transcendentals=0),
    )(value, *others)


def dot(left, right, left_dim=1, right_dim=0):
    return lax.dot_general(
        left, right, (((left_dim,), (right_dim,)), ((), ())), preferred_element_type=F32
    )


def joint(values, *others):
    first = hold(values[0], *values[1:], *others)
    return [first] + [hold(value, first) for value in values[1:]]


def core_sum(other, mine):
    came = [swap(block, SH, 1) for block in other]
    return [(block, one) for block, one in zip(mine, came)]


def add_up(blocks, cut=slice(None)):
    return sum(wide(block[cut]) for block in blocks)


def context_start(mine):
    half = mine[0][0].shape[0] // 2
    if len(mine) != 4 or half % 16:
        return [swap(low(add_up(blocks)), CT, rel) for rel, blocks in enumerate(mine) if rel]
    top, bottom = slice(0, half), slice(half, None)
    upper = [low(add_up(mine[1], top)), low(add_up(mine[3], top))]
    lower = [low(add_up(mine[2], bottom)), low(add_up(mine[3], bottom))]
    return [swap(jnp.stack(upper), CT, 1), swap(jnp.stack(lower), CT, 2)]


def context_end(mine, came, *middle):
    half = mine[0][0].shape[0] // 2
    if len(mine) != 4 or half % 16:
        return add_up(mine[0]) + sum(wide(block) for block in came)
    top, bottom = slice(0, half), slice(half, None)
    upper, lower = joint(came, *middle)
    pass_upper = low(add_up(mine[2], top) + wide(upper[1]))
    pass_lower = low(add_up(mine[1], bottom) + wide(lower[1]))
    upper = add_up(mine[0], top) + wide(upper[0]) + wide(swap(pass_upper, CT, 2))
    lower = add_up(mine[0], bottom) + wide(lower[0]) + wide(swap(pass_lower, CT, 1))
    return jnp.concatenate([upper, lower])


def trade_start(stacked, *middle):
    shard_count, context_count = lax.axis_size(SH), lax.axis_size(CT)
    parts = [stacked[:context_count]]
    for rel in range(1, shard_count):
        parts.append(swap(stacked[rel * context_count : (rel + 1) * context_count], SH, rel))
    parts = jnp.stack(parts)
    return [parts[:, 0]] + [
        swap(hold(parts[:, rel], *middle), CT, rel) for rel in range(1, context_count)
    ]


def tree_info(parent_row):
    slot_count = parent_row.shape[0]
    slot_ids = jnp.arange(slot_count, dtype=jnp.int32)
    reach = (parent_row[:, None] == slot_ids[None, :]) | (slot_ids[:, None] == slot_ids[None, :])
    span = 1
    while span < slot_count:
        reach = jnp.any(reach[:, :, None] & reach[None, :, :], 1)
        span *= 2
    depths = jnp.sum(reach.astype(jnp.int32), 1) - 1
    return (reach, depths)


def rope_tables(positions, head_dim):
    half_dim = head_dim // 2
    frequency = ROPE_BASE ** (-2.0 * jnp.arange(half_dim, dtype=F32) / head_dim)
    angles = positions.astype(F32)[:, None] * frequency[None, :]
    cosine = jnp.concatenate([jnp.cos(angles), jnp.cos(angles)], -1)
    return (cosine, jnp.concatenate([-jnp.sin(angles), jnp.sin(angles)], -1))


def own_slots(chosen, order, first_expert, expert_dev, capacity):
    expert_ids = first_expert + jnp.arange(expert_dev, dtype=jnp.int32)
    hit = chosen[:, :, :, None] == expert_ids
    rank = jnp.sum(jnp.where(hit, order[:, :, :, None], 0), 2)
    routed = jnp.any(hit, 2)
    rank = jnp.where(routed, rank, 2**30).transpose(0, 2, 1)
    routed = routed.transpose(0, 2, 1)
    place = jnp.sum((rank[:, :, None, :] < rank[:, :, :, None]).astype(jnp.int32), -1)
    return jnp.where(routed & (place < capacity), place, -1)


def split_low(value):
    high = low(value)
    return [high, low(value - wide(high))]


def compiler_params():
    return pltpu.CompilerParams(vmem_limit_bytes=VMEM_BYTES)


def cost(microseconds):
    return pl.CostEstimate(
        flops=int(microseconds * 1e9), bytes_accessed=0, transcendentals=0
    )


def column_chunks(width):
    starts = list(range(0, width, CHUNK))
    return [slice(start, min(start + CHUNK, width)) for start in starts]


def choose_matrix(slots, pad):
    count, rows = slots.shape
    places = lax.broadcasted_iota(jnp.int32, (pad, rows), 0)
    parts = [
        jnp.where(slots[one : one + 1, :] == places, 1.0, 0.0) for one in range(count)
    ]
    return low(jnp.concatenate(parts, 0))


def choose_turned(slots, pad):
    count, rows = slots.shape
    expert = lax.broadcasted_iota(jnp.int32, (count, count * pad), 0)
    column = lax.broadcasted_iota(jnp.int32, (count, count * pad), 1)
    inside = (column >= expert * pad) & (column < (expert + 1) * pad)
    spread = dot(low(slots), low(jnp.where(inside, 1.0, 0.0)), 0, 0)
    place = jnp.sum(jnp.where(inside, column - expert * pad, 0), 0, keepdims=True)
    return low(jnp.where(spread == wide(place), 1.0, 0.0))


def load_block(step, blocks, buffer, sems):
    slots = buffer.shape[0]

    def copy(rel):
        return pltpu.make_async_copy(blocks[rel], buffer.at[rel % slots], sems.at[rel % slots])

    for rel in range(len(blocks)):

        @pl.when(step == rel)
        def _():
            if rel == 0:
                for ahead in range(min(slots, len(blocks)) - 1):
                    copy(ahead).start()
            if rel + slots - 1 < len(blocks):
                copy(rel + slots - 1).start()
            copy(rel).wait()


def split_refs(refs):
    parts = []
    for ref in refs:
        parts += [ref] if len(ref.shape) == 2 else [ref.at[one] for one in range(ref.shape[0])]
    return parts


def dispatch_kernel(pad, slots_ref, *refs):
    *blocks, out_ref, buffer, sems = refs
    blocks = split_refs(blocks)
    step = pl.program_id(0)
    load_block(step, blocks, buffer, sems)
    choose = choose_matrix(slots_ref[0], pad)
    count = slots_ref.shape[1]
    for cut in column_chunks(buffer.shape[2]):
        picked = low(dot(choose, buffer[lax.rem(step, buffer.shape[0]), :, cut]))
        for one in range(count):
            out_ref[one, 0, :, cut] = picked[one * pad : (one + 1) * pad]


def dispatch(slots, blocks, pad):
    group_count, expert_dev, rows = slots.shape
    width = blocks[0].shape[1]
    blocks = [array_of(block) for block in blocks if array_of(block) is block or block[1] == 0]
    return pl.pallas_call(
        functools.partial(dispatch_kernel, pad),
        grid=(group_count,),
        out_shape=jax.ShapeDtypeStruct((expert_dev, group_count, pad, width), BF16),
        in_specs=[pl.BlockSpec((1, expert_dev, rows), lambda i: (i, 0, 0))]
        + [pl.BlockSpec(memory_space=pl.ANY)] * len(blocks),
        out_specs=pl.BlockSpec((expert_dev, 1, pad, width), lambda i: (0, i, 0, 0)),
        scratch_shapes=[pltpu.VMEM((4, rows, width), BF16), pltpu.SemaphoreType.DMA((4,))],
        compiler_params=compiler_params(),
        cost_estimate=cost(12),
    )(slots, *blocks)


def combine_all(slots_ref, scratch, pad, outs, buffer, sems):
    count, pair_rows, width = scratch.shape
    group_count = len(outs)

    def copy(turn, source):
        return pltpu.make_async_copy(buffer.at[turn % 2], outs[source], sems.at[turn % 2])

    def body(turn, carry):
        source = lax.rem(turn + group_count // 2, group_count)
        choose = choose_turned(slots_ref[source], pad)
        start = pl.multiple_of(source * pad, pad)

        @pl.when(turn >= 2)
        def _():
            copy(turn, 0).wait()

        for cut in column_chunks(width):
            picked = scratch[:, pl.ds(start, pad), cut].reshape(count * pad, cut.stop - cut.start)
            buffer[turn % 2, :, cut] = low(dot(choose, picked))

        for one in range(group_count):

            @pl.when(source == one)
            def _():
                copy(turn, one).start()

        return carry

    lax.fori_loop(0, group_count, body, 0, unroll=2)
    for turn in range(group_count - 2, group_count):
        copy(turn, 0).wait()


def experts_kernel(
    group_count,
    pad,
    pieces,
    expert_count,
    first_ref,
    slots_ref,
    grads_ref,
    gate_ref,
    up_ref,
    down_ref,
    *refs,
):
    blocks = refs[:group_count]
    rows_out, act_out, back_out = refs[group_count : group_count + 3]
    outs = refs[group_count + 3 : 2 * group_count + 3]
    buffer, row_scratch, back_scratch, gate_scratch, sems, out_sems = refs[2 * group_count + 3 :]
    expert_dev, pair_rows, width = row_scratch.shape
    piece_rows = pair_rows // pieces
    hidden = gate_ref.shape[2]
    step = pl.program_id(0)

    def out_copy(one):
        return pltpu.make_async_copy(row_scratch.at[one], rows_out.at[one], out_sems.at[one])

    def pick(source, carry):
        load_block(source, blocks, buffer, sems)
        choose = choose_matrix(slots_ref[source], pad)
        start = pl.multiple_of(source * pad, pad)
        for cut in column_chunks(width):
            picked = low(dot(choose, buffer[lax.rem(source, buffer.shape[0]), :, cut]))
            for one in range(expert_dev):
                row_scratch[one, pl.ds(start, pad), cut] = picked[one * pad : (one + 1) * pad]
        gates = dot(choose, buffer[lax.rem(source, buffer.shape[0]), :, width:])
        gates = gates[:, :expert_count] + gates[:, expert_count:]
        column = lax.broadcasted_iota(jnp.int32, (pad, expert_count), 1)
        for one in range(expert_dev):
            own = column == first_ref[0] + one
            gate_scratch[one, pl.ds(start, pad), :] = jnp.sum(
                jnp.where(own, gates[one * pad : (one + 1) * pad], 0.0), -1, keepdims=True
            )
        return carry

    @pl.when(step == 0)
    def _():
        lax.fori_loop(0, group_count, pick, 0, unroll=2)

    one = step // pieces
    start = pl.multiple_of(lax.rem(step, pieces) * piece_rows, piece_rows)
    span = pl.ds(start, piece_rows)

    @pl.when(start == 0)
    def _():
        out_copy(one).start()

    rows = row_scratch[one, span, :]
    gate_proj = dot(rows, gate_ref[0])
    up_proj = dot(rows, up_ref[0])
    act_raw = dot(grads_ref[0], down_ref[0], 1, 1)
    gates = gate_scratch[one, span, :]
    sigmoid_gate = 1.0 / (1.0 + jnp.exp(-gate_proj))
    silu_gate = gate_proj * sigmoid_gate
    activated = wide(low(silu_gate * up_proj))
    dots = jnp.sum(activated * act_raw, -1, keepdims=True)
    act_grad = act_raw * gates
    gate_low = low(act_grad * up_proj * sigmoid_gate * (1.0 + gate_proj * (1.0 - sigmoid_gate)))
    up_low = low(act_grad * silu_gate)
    act_out[0] = low(activated * gates)
    back_out[0, :, :hidden] = gate_low
    back_out[0, :, hidden:] = up_low
    for cut in column_chunks(width):
        back_scratch[one, span, cut] = low(
            dot(gate_low, gate_ref[0, cut, :], 1, 1) + dot(up_low, up_ref[0, cut, :], 1, 1)
        )
    column = lax.broadcasted_iota(jnp.int32, (piece_rows, expert_count), 1)
    spread = jnp.where(column == first_ref[0] + one, dots, 0.0)
    back_scratch[one, span, width:] = jnp.concatenate(split_low(spread), 1)

    @pl.when(step == expert_dev * pieces - 1)
    def _():
        combine_all(slots_ref, back_scratch, pad, outs, buffer, sems)
        for one in range(expert_dev):
            out_copy(one).wait()


def experts(first, slots, blocks, grad_rows, w_gate, w_up, w_down, pad, expert_count):
    group_count, expert_dev, rows = slots.shape
    _, width, hidden = w_gate.shape
    pair_rows = group_count * pad
    pieces = max(1, pair_rows // 384)
    piece_rows = pair_rows // pieces
    full = blocks[0].shape[1]
    whole = pl.BlockSpec(slots.shape, lambda i: (0, 0, 0))
    into = pl.BlockSpec((1, width, hidden), lambda i: (i // pieces, 0, 0))
    onto = pl.BlockSpec((1, hidden, width), lambda i: (i // pieces, 0, 0))

    def piece(size):
        return pl.BlockSpec((1, piece_rows, size), lambda i: (i // pieces, lax.rem(i, pieces), 0))

    pairs = expert_dev * pair_rows
    return pl.pallas_call(
        functools.partial(experts_kernel, group_count, pad, pieces, expert_count),
        grid=(expert_dev * pieces,),
        out_shape=[
            jax.ShapeDtypeStruct((expert_dev, pair_rows, size), BF16)
            for size in (width, hidden, 2 * hidden)
        ]
        + [jax.ShapeDtypeStruct((rows, full), BF16)] * group_count,
        in_specs=[pl.BlockSpec(memory_space=pltpu.SMEM), whole, piece(width), into, into, onto]
        + [pl.BlockSpec(memory_space=pl.ANY)] * group_count,
        out_specs=[pl.BlockSpec(memory_space=pl.ANY), piece(hidden), piece(2 * hidden)]
        + [pl.BlockSpec(memory_space=pl.ANY)] * group_count,
        scratch_shapes=[
            pltpu.VMEM((4, rows, full), BF16),
            pltpu.VMEM((expert_dev, pair_rows, width), BF16),
            pltpu.VMEM((expert_dev, pair_rows, full), BF16),
            pltpu.VMEM((expert_dev, pair_rows, 1), F32),
            pltpu.SemaphoreType.DMA((4,)),
            pltpu.SemaphoreType.DMA((expert_dev,)),
        ],
        compiler_params=compiler_params(),
        cost_estimate=cost(100),
    )(first, slots, grad_rows, w_gate, w_up, w_down, *blocks)


def expert_out_kernel(pad, pieces, skip, slots_ref, act_ref, down_ref, *refs):
    outs, (scratch, buffer, sems) = split_refs(refs[skip:-3]), refs[-3:]
    expert_dev, pair_rows, width = scratch.shape
    piece_rows = pair_rows // pieces
    step = pl.program_id(0)
    start = pl.multiple_of(lax.rem(step, pieces) * piece_rows, piece_rows)
    for cut in column_chunks(width):
        scratch[step // pieces, pl.ds(start, piece_rows), cut] = low(
            dot(act_ref[0], down_ref[0, :, cut])
        )

    @pl.when(step == expert_dev * pieces - 1)
    def _():
        combine_all(slots_ref, scratch, pad, outs, buffer, sems)


def expert_out(slots, act, w_down, pad, near, *earlier):
    group_count, expert_dev, rows = slots.shape
    _, hidden, width = w_down.shape
    pair_rows = group_count * pad
    pieces = max(1, pair_rows // 384)
    pairs = expert_dev * pair_rows
    return pl.pallas_call(
        functools.partial(expert_out_kernel, pad, pieces, len(earlier)),
        grid=(expert_dev * pieces,),
        out_shape=[jax.ShapeDtypeStruct((rows, width), BF16)] * near
        + [jax.ShapeDtypeStruct((group_count - near, rows, width), BF16)],
        in_specs=[
            pl.BlockSpec(slots.shape, lambda i: (0, 0, 0)),
            pl.BlockSpec(
                (1, pair_rows // pieces, hidden), lambda i: (i // pieces, lax.rem(i, pieces), 0)
            ),
            pl.BlockSpec((1, hidden, width), lambda i: (i // pieces, 0, 0)),
        ]
        + [pl.BlockSpec(memory_space=pl.ANY)] * len(earlier),
        out_specs=[pl.BlockSpec(memory_space=pl.ANY)] * (near + 1),
        scratch_shapes=[
            pltpu.VMEM((expert_dev, pair_rows, width), BF16),
            pltpu.VMEM((2, rows, width), BF16),
            pltpu.SemaphoreType.DMA((2,)),
        ],
        compiler_params=compiler_params(),
        cost_estimate=cost(40),
    )(slots, act, w_down, *earlier)


def weight_grad_kernel(pieces, skip, left_ref, right_ref, *outs):
    outs = outs[skip:]
    inside = lax.rem(pl.program_id(0), pieces)
    size = outs[0].shape[2]
    tall = left_ref.shape[2] >= right_ref.shape[2]

    def add(out_ref, index, term):
        if pieces == 1:
            out_ref[index] = term
        else:

            @pl.when(inside == 0)
            def _():
                out_ref[index] = term

            @pl.when(inside > 0)
            def _():
                out_ref[index] += term

    if tall:
        for cut in column_chunks(left_ref.shape[2]):
            term = dot(left_ref[0, :, cut], right_ref[0], 0, 0)
            for one, out_ref in enumerate(outs):
                add(out_ref, (0, cut), term[:, one * size : (one + 1) * size])
    else:
        for cut in column_chunks(right_ref.shape[2]):
            add(outs[0], (0, slice(None), cut), dot(left_ref[0], right_ref[0, :, cut], 0, 0))


def weight_grad(left, right, count, *earlier):
    expert_dev, pair_rows, tall = left.shape
    size = right.shape[2] // count
    pieces = max(1, pair_rows // 384)

    def piece(width):
        return pl.BlockSpec(
            (1, pair_rows // pieces, width), lambda i: (i // pieces, lax.rem(i, pieces), 0)
        )

    return pl.pallas_call(
        functools.partial(weight_grad_kernel, pieces, len(earlier)),
        grid=(expert_dev * pieces,),
        out_shape=[jax.ShapeDtypeStruct((expert_dev, tall, size), F32)] * count,
        in_specs=[piece(tall), piece(right.shape[2])]
        + [pl.BlockSpec(memory_space=pl.ANY)] * len(earlier),
        out_specs=[pl.BlockSpec((1, tall, size), lambda i: (i // pieces, 0, 0))] * count,
        compiler_params=compiler_params(),
        cost_estimate=cost(20),
    )(left, right, *earlier)


def scatter_dot_kernel(index_ref, value_ref, *refs):
    blocks, out_ref = refs[:-1], refs[-1]
    depth = blocks[0].shape[0]
    for rel, block in enumerate(blocks):
        start = pl.multiple_of((index_ref[0] ^ rel) * depth, depth)
        part = dot(value_ref[...], block[...], 1, 1)
        out_ref[:, pl.ds(start, depth)] = part.astype(out_ref.dtype)


def scatter_dot(index, value, blocks, cut, kind):
    rows = value.shape[0]
    depth = blocks[0].shape[0]
    size = cut.stop - cut.start
    if depth % 128:
        whole = place_rows([plain(block)[:, cut] for block in blocks], index)
        return dot(value, whole, 1, 1).astype(kind)
    first = cut.start // size
    return pl.pallas_call(
        scatter_dot_kernel,
        grid=(1,),
        out_shape=jax.ShapeDtypeStruct((rows, depth * len(blocks)), kind),
        in_specs=[
            pl.BlockSpec(memory_space=pltpu.SMEM),
            pl.BlockSpec((rows, size), lambda i: (0, 0)),
        ]
        + [block_spec(block, size, first) for block in blocks],
        out_specs=pl.BlockSpec((rows, depth * len(blocks)), lambda i: (0, 0)),
        compiler_params=compiler_params(),
        cost_estimate=cost(12),
    )(index.reshape(1), value, *[array_of(block) for block in blocks])


def attend_kernel(score_scale, context_count, query_ref, bias_ref, *refs):
    blocks = refs[:context_count]
    out_ref, total_ref = refs[context_count:]
    head_dim = query_ref.shape[1]
    scores = jnp.concatenate(
        [dot(query_ref[...], block[:, :head_dim], 1, 1) for block in blocks], 1
    )
    scores = scores * score_scale + bias_ref[...]
    row_peak = jnp.max(scores, -1, keepdims=True)
    weights = jnp.exp(scores - row_peak)
    row_total = jnp.sum(weights, -1, keepdims=True)
    probabilities = low(weights / row_total)
    rows = query_ref.shape[0]
    attended = sum(
        dot(probabilities[:, rel * rows : (rel + 1) * rows], block[:, head_dim:])
        for rel, block in enumerate(blocks)
    )
    out_ref[...] = low(attended)
    total_ref[0] = row_peak + jnp.log(row_total)


def attend(queries, blocks, bias, head_dim):
    rows, head_width = queries.shape
    heads = head_width // head_dim
    one = pl.BlockSpec((rows, head_dim), lambda h: (0, h))
    two = pl.BlockSpec((rows, 2 * head_dim), lambda h: (0, h))
    return pl.pallas_call(
        functools.partial(attend_kernel, head_dim ** (-0.5), len(blocks)),
        grid=(heads,),
        out_shape=[
            jax.ShapeDtypeStruct((rows, head_width), BF16),
            jax.ShapeDtypeStruct((heads, rows, 1), F32),
        ],
        in_specs=[one, pl.BlockSpec(bias.shape, lambda h: (0, 0))] + [two] * len(blocks),
        out_specs=[one, pl.BlockSpec((1, rows, 1), lambda h: (h, 0, 0))],
        compiler_params=compiler_params(),
        cost_estimate=cost(12),
    )(queries, bias, *blocks)


def attend_back_kernel(score_scale, context_count, query_ref, grad_ref, total_ref, bias_ref, *refs):
    blocks = refs[:context_count]
    query_out, outs = refs[context_count], refs[context_count + 1 :]
    rows, head_dim = query_ref.shape
    query, grad = query_ref[...], grad_ref[...]
    scores = jnp.concatenate([dot(query, block[:, :head_dim], 1, 1) for block in blocks], 1)
    probabilities = jnp.exp(scores * score_scale + bias_ref[...] - total_ref[0])
    prob_grad = jnp.concatenate([dot(grad, block[:, head_dim:], 1, 1) for block in blocks], 1)
    score_grad = probabilities * (
        prob_grad - jnp.sum(probabilities * prob_grad, -1, keepdims=True)
    )
    score_low = low(score_grad * score_scale)
    prob_low = low(probabilities)
    query_grad = jnp.zeros((rows, head_dim), F32)
    for rel, (block, out) in enumerate(zip(blocks, outs)):
        cut = slice(rel * rows, (rel + 1) * rows)
        query_grad = query_grad + dot(score_low[:, cut], block[:, :head_dim])
        out[:, :head_dim] = low(dot(score_low[:, cut], query, 0, 0))
        out[:, head_dim:] = low(dot(prob_low[:, cut], grad, 0, 0))
    query_out[...] = query_grad


def attend_back(queries, grads, totals, blocks, bias, head_dim):
    rows, head_width = queries.shape
    heads = head_width // head_dim
    one = pl.BlockSpec((rows, head_dim), lambda h: (0, h))
    two = pl.BlockSpec((rows, 2 * head_dim), lambda h: (0, h))
    return pl.pallas_call(
        functools.partial(attend_back_kernel, head_dim ** (-0.5), len(blocks)),
        grid=(heads,),
        out_shape=[jax.ShapeDtypeStruct((rows, head_width), F32)]
        + [jax.ShapeDtypeStruct((rows, 2 * head_width), BF16)] * len(blocks),
        in_specs=[
            one,
            one,
            pl.BlockSpec((1, rows, 1), lambda h: (h, 0, 0)),
            pl.BlockSpec(bias.shape, lambda h: (0, 0)),
        ]
        + [two] * len(blocks),
        out_specs=[one] + [two] * len(blocks),
        compiler_params=compiler_params(),
        cost_estimate=cost(12),
    )(queries, grads, totals, bias, *blocks)


def row_norm(values):
    return lax.rsqrt(jnp.mean(values * values, -1, keepdims=True) + EPS)


def chunk(index_ref, rel, size):
    return pl.ds(pl.multiple_of((index_ref[0] ^ rel) * size, size), size)


def whole_spec(value):
    return pl.BlockSpec(value.shape, lambda i: (0,) * value.ndim)


def column_spec(value, size, first=0):
    return pl.BlockSpec((value.shape[0], size), lambda i: (0, first + i))


def project_kernel(group_count, heads, index_ref, hidden_ref, *refs):
    smalls, blocks = refs[:group_count], refs[group_count : 2 * group_count]
    attn_ref, out_ref, square_ref, scale_ref, moe_ref, gain_ref = refs[2 * group_count :]
    depth = blocks[0].shape[0]
    piece = gain_ref.shape[1] // (2 * heads * group_count)
    used = 2 * heads * piece

    @pl.when(pl.program_id(0) == 0)
    def _():
        scale = row_norm(wide(hidden_ref[...]))
        scale_ref[...] = scale
        gains = jnp.zeros(gain_ref.shape, F32)
        for rel, small in enumerate(smalls):
            cut = chunk(index_ref, rel, depth)
            columns = wide(small[...]).T
            attn_ref[:, cut] = low(wide(hidden_ref[:, cut]) * scale * columns[0:1, :])
            moe_ref[:, cut] = columns[0:2, :]
            row = lax.broadcasted_iota(jnp.int32, (depth, gain_ref.shape[1]), 0)
            column = lax.broadcasted_iota(jnp.int32, (depth, gain_ref.shape[1]), 1)
            inside = column - (index_ref[0] ^ rel) * piece - (row // piece) * piece * group_count
            place = (inside == lax.rem(row, piece)) & (row < used)
            gains = gains + dot(low(columns), low(jnp.where(place, 1.0, 0.0)))[2:3, :]
        gain_ref[...] = gains

    total = jnp.zeros(out_ref.shape, F32)
    for rel, block in enumerate(blocks):
        total = total + dot(attn_ref[:, chunk(index_ref, rel, depth)], block[...])
    out_ref[...] = total
    square_ref[0] = jnp.sum(total * total, -1, keepdims=True)


def project(index, hidden, blocks, tile, heads):
    rows, width = hidden.shape
    depth = blocks[0].shape[0]
    count = len(blocks)
    if depth % 128:
        packed = place_rows(blocks, index)
        hidden = wide(hidden)
        scale = row_norm(hidden)
        attn_in = low(hidden * scale * wide(packed[:, 3 * tile]))
        projected = dot(attn_in, packed[:, : 3 * tile])
        squares = jnp.sum((projected * projected).reshape(rows, 3, tile), -1).T
        norm_gains = wide(packed[:, 3 * tile : 3 * tile + 2]).T
        gains = wide(packed[:, 3 * tile + 2]).reshape(count, depth)[:, : 2 * tile // count]
        gains = gains.reshape(count, 2, heads, -1).transpose(1, 2, 0, 3).reshape(2, tile)
        return attn_in, projected, squares, scale, norm_gains, gains
    attn_in, projected, squares, scale, norm_gains, gains = pl.pallas_call(
        functools.partial(project_kernel, count, heads),
        grid=(3,),
        out_shape=[
            jax.ShapeDtypeStruct((rows, width), BF16),
            jax.ShapeDtypeStruct((rows, 3 * tile), F32),
            jax.ShapeDtypeStruct((3, rows, 1), F32),
            jax.ShapeDtypeStruct((rows, 1), F32),
            jax.ShapeDtypeStruct((2, width), F32),
            jax.ShapeDtypeStruct((1, 2 * tile), F32),
        ],
        in_specs=[pl.BlockSpec(memory_space=pltpu.SMEM), whole_spec(hidden)]
        + [pl.BlockSpec((depth, 128), lambda i: (0, 3 * tile // 128))] * count
        + [column_spec(blocks[0], tile)] * count,
        out_specs=[
            whole_spec(hidden),
            pl.BlockSpec((rows, tile), lambda i: (0, i)),
            pl.BlockSpec((1, rows, 1), lambda i: (i, 0, 0)),
            pl.BlockSpec((rows, 1), lambda i: (0, 0)),
            pl.BlockSpec((2, width), lambda i: (0, 0)),
            pl.BlockSpec((1, 2 * tile), lambda i: (0, 0)),
        ],
        compiler_params=compiler_params(),
        cost_estimate=cost(12),
    )(index.reshape(1), hidden, *blocks, *blocks)
    return attn_in, projected, squares[:, :, 0], scale, norm_gains, gains.reshape(2, tile)


def swapped(values):
    half = values.shape[1] // 2
    return jnp.concatenate([values[:, half:], values[:, :half]], 1)


def turn_kernel(query_ref, key_ref, value_ref, scale_ref, gain_ref, cos_ref, sin_ref, *outs):
    query_out, pair_out = outs
    size = query_ref.shape[1]
    for part, (source, out_ref) in enumerate([(query_ref, query_out), (key_ref, pair_out)]):
        hat = source[...] * scale_ref[part] * gain_ref[part : part + 1, :]
        out_ref[:, :size] = low(hat * cos_ref[...] + swapped(hat) * sin_ref[...])
    pair_out[:, size:] = low(value_ref[...])


def turn_heads(projected, scales, gains, cosine, sine, heads):
    rows, size = cosine.shape
    return pl.pallas_call(
        turn_kernel,
        grid=(heads,),
        out_shape=[
            jax.ShapeDtypeStruct((rows, heads * size), BF16),
            jax.ShapeDtypeStruct((rows, 2 * heads * size), BF16),
        ],
        in_specs=[column_spec(projected, size, part * heads) for part in range(3)]
        + [whole_spec(scales), column_spec(gains, size), whole_spec(cosine), whole_spec(sine)],
        out_specs=[
            pl.BlockSpec((rows, size), lambda i: (0, i)),
            pl.BlockSpec((rows, 2 * size), lambda i: (0, i)),
        ],
        compiler_params=compiler_params(),
        cost_estimate=cost(6),
    )(projected, projected, projected, scales, gains, cosine, sine)


def turn_back_kernel(part_count, *refs):
    query_grad, parts = refs[0], refs[1 : 1 + part_count]
    query_ref, key_ref, scale_ref, gain_ref, cos_ref, sin_ref = refs[1 + part_count : 7 + part_count]
    query_out, key_out, value_out, inner_out, gain_out = refs[7 + part_count :]
    size = query_ref.shape[1]
    total = sum(wide(part[...]) for part in parts)
    value_out[...] = low(total[:, size:])
    pairs = [(query_grad[...], query_ref, query_out), (total[:, :size], key_ref, key_out)]
    for part, (grad, source, out_ref) in enumerate(pairs):
        hat = source[...] * scale_ref[part]
        norm_grad = grad * cos_ref[...] - swapped(grad) * sin_ref[...]
        gain_out[part : part + 1, :] = jnp.sum(norm_grad * hat, 0, keepdims=True)
        hat_grad = norm_grad * gain_ref[part : part + 1, :]
        out_ref[...] = hat_grad
        inner = jnp.sum(hat_grad * hat, -1, keepdims=True)

        @pl.when(pl.program_id(0) == 0)
        def _():
            inner_out[part] = inner

        @pl.when(pl.program_id(0) > 0)
        def _():
            inner_out[part] += inner


def turn_back(query_grad, parts, projected, scales, gains, cosine, sine, heads):
    rows, size = cosine.shape
    one = pl.BlockSpec((rows, size), lambda i: (0, i))
    two = pl.BlockSpec((rows, 2 * size), lambda i: (0, i))
    return pl.pallas_call(
        functools.partial(turn_back_kernel, len(parts)),
        grid=(heads,),
        out_shape=[jax.ShapeDtypeStruct((rows, heads * size), kind) for kind in (F32, F32, BF16)]
        + [
            jax.ShapeDtypeStruct((2, rows, 1), F32),
            jax.ShapeDtypeStruct((2, heads * size), F32),
        ],
        in_specs=[one]
        + [two] * len(parts)
        + [column_spec(projected, size, part * heads) for part in range(2)]
        + [whole_spec(scales), column_spec(gains, size), whole_spec(cosine), whole_spec(sine)],
        out_specs=[
            one,
            one,
            one,
            pl.BlockSpec((2, rows, 1), lambda i: (0, 0, 0)),
            pl.BlockSpec((2, size), lambda i: (0, i)),
        ],
        compiler_params=compiler_params(),
        cost_estimate=cost(8),
    )(query_grad, *parts, projected, projected, scales, gains, cosine, sine)


def input_grad_kernel(*refs):
    index_ref, query_grad, key_grad, value_low, projected, scale_ref, inner_ref = refs[:7]
    blocks, (low_ref, part_ref) = refs[7:-2], refs[-2:]
    size = query_grad.shape[1]
    depth = blocks[0].shape[0]
    for part, grad in enumerate([query_grad, key_grad]):
        cut = slice(part * size, (part + 1) * size)
        hat = projected[:, cut] * scale_ref[part]
        low_ref[:, cut] = low(scale_ref[part] * (grad[...] - hat * inner_ref[part]))
    low_ref[:, 2 * size :] = value_low[...]
    for rel, block in enumerate(blocks):
        part_ref[:, chunk(index_ref, rel, depth)] = low(dot(low_ref[...], block[...], 1, 1))


def input_grad(index, query_grad, key_grad, value_low, projected, scales, inner, blocks):
    rows, size = query_grad.shape
    depth = blocks[0].shape[0]
    if depth % 128:
        parts = []
        for part, grad in enumerate([query_grad, key_grad]):
            hat = projected[:, part * size : (part + 1) * size] * scales[part]
            parts.append(low(scales[part] * (grad - hat * inner[part])))
        qkv_low = jnp.concatenate(parts + [value_low], 1)
        return qkv_low, low(dot(qkv_low, place_rows(blocks, index)[:, : 3 * size], 1, 1))
    weights = pl.BlockSpec((depth, 3 * size), lambda i: (0, 0))
    values = [query_grad, key_grad, value_low, projected, scales, inner]
    return pl.pallas_call(
        input_grad_kernel,
        grid=(1,),
        out_shape=[
            jax.ShapeDtypeStruct((rows, 3 * size), BF16),
            jax.ShapeDtypeStruct((rows, depth * len(blocks)), BF16),
        ],
        in_specs=[pl.BlockSpec(memory_space=pltpu.SMEM)]
        + [whole_spec(value) for value in values]
        + [weights] * len(blocks),
        out_specs=[
            pl.BlockSpec((rows, 3 * size), lambda i: (0, 0)),
            pl.BlockSpec((rows, depth * len(blocks)), lambda i: (0, 0)),
        ],
        compiler_params=compiler_params(),
        cost_estimate=cost(12),
    )(index.reshape(1), *values, *blocks)


def route_kernel(tensor_count, expert_count, index_ref, tensor_ref, gain_ref, *refs):
    parts, routers = refs[:tensor_count], refs[tensor_count:-4]
    sent_ref, probs_ref, residual_ref, scale_ref = refs[-4:]
    quarter = parts[0].shape[1]
    rows, width = residual_ref.shape
    depth = routers[0].shape[0]
    for rel, part in enumerate(parts):
        residual_ref[:, chunk(tensor_ref, rel, quarter)] = part[...]
    residual = wide(residual_ref[...])
    scale = row_norm(residual)
    scale_ref[...] = scale
    sent_ref[:, :width] = low(residual * scale * gain_ref[...])
    logits = jnp.zeros((rows, routers[0].shape[1]), F32)
    for rel, router in enumerate(routers):
        logits = logits + dot(sent_ref[:, chunk(index_ref, rel, depth)], router[...])
    logits = logits[:, :expert_count]
    exponent = jnp.exp(logits - jnp.max(logits, -1, keepdims=True))
    probs = exponent / jnp.sum(exponent, -1, keepdims=True)
    probs_ref[...] = probs
    sent_ref[:, width:] = jnp.concatenate(split_low(probs), 1)


def route(index, tensor_index, gain, parts, blocks, cut, expert_count):
    rows, quarter = parts[0].shape
    width = quarter * len(parts)
    depth = blocks[0].shape[0]
    if depth % 128:
        residual = jnp.concatenate(in_order(parts, tensor_index), 1)
        scale = row_norm(wide(residual))
        moe_in = low(wide(residual) * scale * gain)
        logits = dot(moe_in, place_rows([plain(block)[:, cut] for block in blocks], index))
        logits = logits[:, :expert_count]
        exponent = jnp.exp(logits - jnp.max(logits, -1, keepdims=True))
        probs = exponent / jnp.sum(exponent, -1, keepdims=True)
        return jnp.concatenate([moe_in] + split_low(probs), 1), probs, residual, scale
    size = cut.stop - cut.start
    shapes = [(width + 2 * expert_count, BF16), (expert_count, F32), (width, BF16), (1, F32)]
    scalar = pl.BlockSpec(memory_space=pltpu.SMEM)
    return pl.pallas_call(
        functools.partial(route_kernel, len(parts), expert_count),
        grid=(1,),
        out_shape=[jax.ShapeDtypeStruct((rows, one), kind) for one, kind in shapes],
        in_specs=[scalar, scalar, whole_spec(gain)]
        + [whole_spec(part) for part in parts]
        + [block_spec(block, size, cut.start // size) for block in blocks],
        out_specs=[pl.BlockSpec((rows, one), lambda i: (0, 0)) for one, _ in shapes],
        compiler_params=compiler_params(),
        cost_estimate=cost(8),
    )(index.reshape(1), tensor_index.reshape(1), gain, *parts, *[array_of(b) for b in blocks])


def residual_kernel(tensor_count, group_count, index_ref, tensor_ref, *refs):
    gain_ref, logit_ref, residual_ref, scale_ref, grad_ref = refs[:5]
    parts, refs = refs[5 : 5 + tensor_count], refs[5 + tensor_count :]
    routers, blocks = refs[:group_count], refs[group_count : 2 * group_count]
    low_ref, share_ref, gain_out, heads_ref, scratch = refs[2 * group_count :]
    quarter = parts[0].shape[1]
    depth = blocks[0].shape[0]
    for rel, part in enumerate(parts):
        scratch[:, chunk(tensor_ref, rel, quarter)] = wide(part[...])
    for rel, router in enumerate(routers):
        scratch[:, chunk(index_ref, rel, depth)] += dot(logit_ref[...], router[...], 1, 1)
    normed = wide(residual_ref[...]) * scale_ref[...]
    gain_out[...] = jnp.sum(scratch[...] * normed, 0, keepdims=True)
    normed_grad = scratch[...] * gain_ref[...]
    mean = jnp.mean(normed_grad * normed, -1, keepdims=True)
    scratch[...] = wide(grad_ref[...]) + scale_ref[...] * (normed_grad - normed * mean)
    low_ref[...] = low(scratch[...])
    share_ref[...] = scratch[:, chunk(tensor_ref, 0, quarter)]
    total = jnp.zeros(heads_ref.shape, F32)
    for rel, block in enumerate(blocks):
        total = total + dot(low_ref[:, chunk(index_ref, rel, depth)], block[...])
    heads_ref[...] = low(total)


def residual_back(index, tensor_index, gain, logit, residual, scale, grad, parts, blocks, heads, cut):
    rows, quarter = parts[0].shape
    width = quarter * len(parts)
    depth = blocks[0].shape[0]
    if depth % 128:
        whole = place_rows([plain(block) for block in blocks], index)
        moe_in_grad = wide(jnp.concatenate(in_order(parts, tensor_index), 1))
        moe_in_grad = moe_in_grad + dot(logit, whole[:, cut], 1, 1)
        normed = wide(residual) * scale
        gain_grad = jnp.sum(moe_in_grad * normed, 0, keepdims=True)
        normed_grad = moe_in_grad * gain
        mean = jnp.mean(normed_grad * normed, -1, keepdims=True)
        total = wide(grad) + scale * (normed_grad - normed * mean)
        share = lax.dynamic_slice_in_dim(total, tensor_index * quarter, quarter, 1)
        return low(total), share, gain_grad, low(dot(low(total), whole[:, :heads]))
    size = cut.stop - cut.start
    shapes = [(rows, width, BF16), (rows, quarter, F32), (1, width, F32), (rows, heads, BF16)]
    scalar = pl.BlockSpec(memory_space=pltpu.SMEM)
    values = [gain, logit, residual, scale, grad] + parts
    arrays = [array_of(block) for block in blocks]
    return pl.pallas_call(
        functools.partial(residual_kernel, len(parts), len(blocks)),
        grid=(1,),
        out_shape=[jax.ShapeDtypeStruct((one, two), kind) for one, two, kind in shapes],
        in_specs=[scalar, scalar]
        + [whole_spec(value) for value in values]
        + [block_spec(block, size, cut.start // size) for block in blocks]
        + [block_spec(block, heads, 0) for block in blocks],
        out_specs=[pl.BlockSpec((one, two), lambda i: (0, 0)) for one, two, _ in shapes],
        scratch_shapes=[pltpu.VMEM((rows, width), F32)],
        compiler_params=compiler_params(),
        cost_estimate=cost(12),
    )(index.reshape(1), tensor_index.reshape(1), *values, *arrays, *arrays)


def late_dot_kernel(part_count, index_ref, *refs):
    traded, late = refs[:part_count], refs[part_count : 2 * part_count]
    blocks, (out_ref, router_ref) = refs[2 * part_count : -2], refs[-2:]
    tall, size = out_ref.shape
    total, router = jnp.zeros(out_ref.shape, F32), jnp.zeros(router_ref.shape, F32)
    for rel, block in enumerate(blocks):
        right = late[rel % part_count][rel // part_count]
        left = traded[rel % part_count][rel // part_count, :, :tall]
        total = total + dot(left, right[:, :size], 0, 0)
        router = router + dot(block[...], right[:, size:], 0, 0)
    out_ref[...] = total
    router_ref[...] = router


def late_dots(index, traded, late, blocks, tall, size):
    rows = blocks[0].shape[0]
    experts = late[0].shape[2] - size
    if size % 128:
        shard_count = traded[0].shape[0]
        left = jnp.concatenate([part[one] for one in range(shard_count) for part in traded])
        right = jnp.concatenate([part[one] for one in range(shard_count) for part in late])
        inputs = [lax.dynamic_slice_in_dim(block, index * size, size, 1) for block in blocks]
        out_grad = dot(left[:, :tall], right[:, :size], 0, 0)
        return out_grad, dot(jnp.concatenate(inputs), right[:, size:], 0, 0)
    return pl.pallas_call(
        functools.partial(late_dot_kernel, len(traded)),
        grid_spec=pltpu.PrefetchScalarGridSpec(
            num_scalar_prefetch=1,
            grid=(1,),
            in_specs=[pl.BlockSpec(one.shape, lambda i, s: (0, 0, 0)) for one in traded + late]
            + [pl.BlockSpec((rows, size), lambda i, s: (0, s[0]))] * len(blocks),
            out_specs=[
                pl.BlockSpec((tall, size), lambda i, s: (0, 0)),
                pl.BlockSpec((size, experts), lambda i, s: (0, 0)),
            ],
        ),
        out_shape=[
            jax.ShapeDtypeStruct((tall, size), F32),
            jax.ShapeDtypeStruct((size, experts), F32),
        ],
        compiler_params=compiler_params(),
        cost_estimate=cost(6),
    )(index.reshape(1), *traded, *late, *blocks)


def qkv_dot_kernel(part_count, first, *refs):
    traded, grads, outs = refs[:part_count], refs[part_count:-3], refs[-3:]
    size = outs[0].shape[1]
    for one, out_ref in enumerate(outs):
        total = jnp.zeros(out_ref.shape, F32)
        for rel, grad in enumerate(grads):
            left = traded[rel % part_count][rel // part_count, :, first:]
            total = total + dot(left, grad[:, one * size : (one + 1) * size], 0, 0)
        out_ref[...] = total


def qkv_dots(traded, grads, first, size):
    tall = traded[0].shape[2] - first
    if tall % 128:
        shard_count = traded[0].shape[0]
        left = jnp.concatenate([part[one] for one in range(shard_count) for part in traded])
        total = dot(left[:, first:], jnp.concatenate(grads), 0, 0)
        return [total[:, one * size : (one + 1) * size] for one in range(3)]
    return pl.pallas_call(
        functools.partial(qkv_dot_kernel, len(traded), first),
        grid=(1,),
        out_shape=[jax.ShapeDtypeStruct((tall, size), F32)] * 3,
        in_specs=[whole_spec(one) for one in traded + grads],
        out_specs=[pl.BlockSpec((tall, size), lambda i: (0, 0))] * 3,
        compiler_params=compiler_params(),
        cost_estimate=cost(8),
    )(*traded, *grads)


def per_device(
    tokens,
    parents,
    routes,
    pair_order,
    norm_attn,
    w_query,
    w_key,
    w_value,
    q_gain,
    k_gain,
    w_out,
    norm_moe,
    w_router,
    w_gate,
    w_up,
    w_down,
    out_grad,
):
    shard_index, context_index, tensor_index = (lax.axis_index(a) for a in (SH, CT, TS))
    context_count, tensor_count = lax.axis_size(CT), lax.axis_size(TS)
    group_count = lax.axis_size(SH) * context_count
    group = shard_index * context_count + context_index
    seg_dev, seg_len, quarter = tokens.shape[1:]
    rows = seg_dev * seg_len
    model_width = quarter * tensor_count
    slice_width = norm_attn.shape[0]
    top_count = routes.shape[3]
    expert_count = w_router.shape[1]
    expert_dev = w_gate.shape[0]
    local_heads, head_dim = q_gain.shape[0], q_gain.shape[1] * group_count
    head_width = local_heads * head_dim
    capacity = tensor_count * (
        (5 * rows * top_count + 4 * expert_count * tensor_count - 1)
        // (4 * expert_count * tensor_count)
    )
    score_scale = head_dim ** (-0.5)

    out_cut = slice(0, head_width)
    router_pad = -expert_count % 128
    router_cut = slice(head_width, head_width + expert_count + router_pad)
    gain_size = q_gain.size
    gain_values = jnp.concatenate([q_gain.reshape(-1), k_gain.reshape(-1)])
    gain_values = jnp.pad(gain_values, (0, slice_width - 2 * gain_size))
    base = 64
    order = jnp.arange(seg_dev, dtype=jnp.int32)[:, None] * (seg_len * top_count) + pair_order[0]
    order = order.reshape(rows, top_count)
    codes = jnp.concatenate([routes.reshape(rows, top_count), order // base, order % base], 1)
    codes = low(codes).reshape(slice_width, -1)
    columns = jnp.stack([norm_attn, norm_moe, gain_values], 1)
    columns = jnp.concatenate([columns, codes], 1)
    columns = jnp.pad(columns, ((0, 0), (0, 128 - columns.shape[1])))
    packed = jnp.concatenate([w_query, w_key, w_value, columns], 1)
    token_parts = around(hold(tokens.reshape(rows, quarter), packed), TS)
    grad_parts = double(hold(out_grad.reshape(1, rows, quarter), *token_parts[1:]), TS)
    qkv_blocks = gather_groups(packed, *token_parts[1:])
    hidden_in = jnp.concatenate(in_order(token_parts, tensor_index), 1)
    grad_output = jnp.concatenate(in_order(grad_parts, tensor_index), 1)

    first_code = 3 * head_width + 3
    codes = [block[:, first_code : first_code + codes.shape[1]] for block in qkv_blocks]
    codes = jnp.stack(codes).reshape(group_count, rows, 3, top_count).astype(jnp.int32)
    slots = own_slots(
        codes[:, :, 0],
        codes[:, :, 1] * base + codes[:, :, 2],
        group * expert_dev,
        expert_dev,
        capacity,
    )
    pad = -(-capacity // 16) * 16

    reachable, depths = tree_info(parents[0])
    first_slot = context_index * seg_dev
    local_depth = lax.dynamic_slice_in_dim(depths, first_slot, seg_dev, 0)
    offsets = jnp.arange(seg_len, dtype=jnp.int32)
    positions = (local_depth[:, None] * seg_len + offsets[None, :]).reshape(rows)
    cosine, sine = rope_tables(positions, head_dim)
    reach_local = lax.dynamic_slice_in_dim(reachable, first_slot, seg_dev, 0)
    masks = []
    for rel in range(context_count):
        other_slot = (context_index ^ rel) * seg_dev
        seen = lax.dynamic_slice_in_dim(reach_local, other_slot, seg_dev, 1)
        seen = seen[:, None, :, None]
        if rel == 0:
            same = jnp.eye(seg_dev, dtype=bool)[:, None, :, None]
            seen = seen & (~same | (offsets[None, :] <= offsets[:, None])[None, :, None, :])
        masks.append(jnp.broadcast_to(seen, (seg_dev, seg_len, seg_dev, seg_len)).reshape(rows, rows))
    bias = jnp.where(jnp.concatenate(masks, 1), 0.0, NEG_FILL)

    attn_in, projected, squares, scale_attn, norm_gains, gains = project(
        group, hidden_in, qkv_blocks, head_width, local_heads
    )
    gain_attn, gain_moe = norm_gains[0], norm_gains[1:]
    out_blocks = jnp.concatenate([w_out.T, jnp.pad(w_router, ((0, 0), (0, router_pad)))], 1)
    out_blocks = hold(out_blocks, qkv_blocks[context_count - 1])
    out_blocks = stack_far(gather_context(out_blocks, projected))
    squares = sum(around(squares[:2], TS))
    scales = lax.rsqrt(squares / model_width + EPS)[:, :, None]
    scales = hold(scales, grad_parts)
    query_rot, key_value = turn_heads(projected, scales, gains, cosine, sine, local_heads)
    key_value = gather_context(hold(key_value, *out_blocks[1:context_count]))
    query_rot = hold(query_rot, slots)
    attended_low, log_total = attend(query_rot, key_value, bias, head_dim)

    def tensor_parts(value):
        return [
            lax.dynamic_slice_in_dim(value, (tensor_index ^ rel) * quarter, quarter, 1)
            for rel in range(tensor_count)
        ]

    def tensor_sum(parts):
        total = wide(parts[0])
        for rel in range(1, tensor_count):
            total = total + wide(swap(low(parts[rel]), TS, rel))
        return total

    attn_part = scatter_dot(group, attended_low, out_blocks, out_cut, BF16)
    attn_share = tensor_sum(tensor_parts(attn_part))
    residual_share = wide(tokens.reshape(rows, quarter)) + attn_share
    grad_blocks = gather_context(hold(grad_output, *key_value[1:]), residual_share)
    parts = around(low(residual_share), TS)
    parts[-1] = hold(parts[-1], grad_blocks[-1])
    sent, router_probs, residual, scale_moe = route(
        group, tensor_index, gain_moe, parts, out_blocks, router_cut, expert_count
    )
    moe_in = sent[:, :model_width]
    grad_blocks = stack_far(grad_blocks[:-1] + [hold(grad_blocks[-1], sent)])
    grad_rows = dispatch(slots, grad_blocks, pad)
    blocks = gather_groups(sent, grad_rows)
    grad_rows = grad_rows.reshape(expert_dev, group_count * pad, model_width)

    def slices(value):
        return [
            lax.dynamic_slice_in_dim(value, (group ^ rel) * slice_width, slice_width, 1)
            for rel in range(group_count)
        ]

    late = hold(jnp.concatenate([attended_low, attn_in], 1), blocks[1])
    traded = [jnp.concatenate([late[:, :head_width], one], 1) for one in slices(late[:, head_width:])]
    traded = trade_start(jnp.stack(traded), blocks[-1])
    first = (group * expert_dev).reshape(1)
    pair_rows, act_gated, pair_back, *row_parts = experts(
        first,
        slots,
        blocks,
        grad_rows,
        w_gate,
        w_up,
        w_down,
        pad,
        expert_count,
    )
    row_far = joint(row_parts[context_count:], *traded[1:])
    row_own = core_sum(row_far, row_parts[:context_count])
    row_came = context_start(row_own)
    *mixed_near, mixed_far = expert_out(
        slots, act_gated, w_down, pad, context_count, *[block[1] for block in row_own[1:]]
    )
    row_total = context_end(row_own, row_came, mixed_near[0])
    (down_grad,) = weight_grad(act_gated, grad_rows, 1, row_total)
    mixed_far = swap(mixed_far, SH, 1)
    (down_grad,) = weight_grad(act_gated, grad_rows, 1, row_total)

    row_low = low(row_total)
    parts = [
        jnp.concatenate([part, row_low[:, model_width:]], 1)
        for part in tensor_parts(row_low[:, :model_width])
    ]
    parts = [parts[0]] + [swap(parts[rel], TS, rel) for rel in range(1, tensor_count)]
    parts[-1] = hold(parts[-1], down_grad, mixed_far)
    row_share = sum(wide(part[:, :quarter]) for part in parts)
    gate_w_grad, up_w_grad = weight_grad(pair_rows, pair_back, 2, row_share)
    prob_grads = sum(wide(part[:, quarter:]) for part in in_order(parts, tensor_index))
    prob_grads = prob_grads[:, :expert_count] + prob_grads[:, expert_count:]
    logit_low = low(
        router_probs * (prob_grads - jnp.sum(prob_grads * router_probs, -1, keepdims=True))
    )
    mixed_far = hold(mixed_far, row_share)
    mixed_own = [(block, mixed_far[one]) for one, block in enumerate(mixed_near)]
    mixed_came = context_start(mixed_own)
    parts = around(low(row_share), TS)
    parts[-1] = hold(parts[-1], gate_w_grad, *mixed_came)
    logit_wide = jnp.pad(logit_low, ((0, 0), (0, router_pad)))
    residual_low, residual_share_grad, gain_moe_grad, grad_heads = residual_back(
        group,
        tensor_index,
        gain_moe,
        logit_wide,
        residual,
        scale_moe,
        grad_output,
        parts,
        out_blocks,
        head_width,
        router_cut,
    )
    mixed_total = context_end(mixed_own, mixed_came, gate_w_grad)
    query_grad, *key_value_grad = attend_back(
        query_rot, grad_heads, log_total, key_value, bias, head_dim
    )
    key_value_grad[-1] = hold(key_value_grad[-1], mixed_total)
    traded_late = [jnp.concatenate([one, logit_low], 1) for one in slices(residual_low)]
    key_value_grad = [(block,) for block in key_value_grad]
    key_value_grad = context_end(key_value_grad, context_start(key_value_grad))
    traded_late = trade_start(jnp.stack(traded_late), key_value_grad)
    key_value_grad = [key_value_grad]
    query_hat_grad, key_hat_grad, value_low, inner, gain_grads = turn_back(
        query_grad, key_value_grad, projected, scales, gains, cosine, sine, local_heads
    )
    inner = butterfly(inner[:, :, 0], TS)[:, :, None] / model_width
    inner = hold(inner, *traded_late[1:])
    qkv_low, attn_part = input_grad(
        group, query_hat_grad, key_hat_grad, value_low, projected, scales, inner, qkv_blocks
    )
    traded_late[0] = hold(traded_late[0], qkv_low)
    out_w_grad, router_grad = late_dots(
        group, traded, traded_late, blocks, head_width, slice_width
    )
    qkv_grads = gather_groups(qkv_low)
    attn_share = tensor_sum(tensor_parts(attn_part))
    attn_share = hold(attn_share, *qkv_grads[1:context_count])
    hidden_share = wide(tokens.reshape(rows, quarter))
    normed_share = hidden_share * scale_attn
    normed_in_grad = attn_share * lax.dynamic_slice_in_dim(gain_attn, tensor_index * quarter, quarter)
    inner = jnp.sum(normed_in_grad * normed_share, -1)
    ends = jnp.zeros((rows + model_width,), F32)
    ends = lax.dynamic_update_slice_in_dim(
        ends, jnp.sum(attn_share * normed_share, 0), rows + tensor_index * quarter, 0
    )
    ends = butterfly(lax.dynamic_update_slice_in_dim(ends, inner, 0, 0), TS)
    inner = ends[:rows, None] / model_width
    gain_attn_grad = ends[rows:]
    mixed_share = tensor_sum(tensor_parts(hold(mixed_total, attn_share)))
    mixed_out = low(residual_share + mixed_share).reshape(tokens.shape)
    traded[0] = hold(traded[0], out_w_grad, mixed_share)
    qkv_w_grads = qkv_dots(traded, qkv_grads, head_width, head_width)
    tokens_grad = residual_share_grad + scale_attn * (normed_in_grad - normed_share * inner)

    gain_grads = gain_grads.reshape(2, local_heads, group_count, -1)
    gain_grads = gain_grads.transpose(2, 0, 1, 3).reshape(group_count, 2 * gain_size)
    vectors = jnp.concatenate(
        [
            gain_attn_grad.reshape(group_count, slice_width),
            gain_moe_grad.reshape(group_count, slice_width),
            gain_grads,
        ],
        1,
    )
    vectors = jnp.concatenate(
        [
            lax.dynamic_slice_in_dim(vectors, group ^ rel, 1, 0)[:, None]
            for rel in range(group_count)
        ]
    )
    vectors = core_sum([vectors[context_count:]], [vectors[:context_count]])
    vectors = add_up(vectors[0])
    vectors = vectors[0] + sum(swap(vectors[rel], CT, rel) for rel in range(1, context_count))
    vectors = vectors[0]
    gain_grads = vectors[2 * slice_width :].reshape((2,) + q_gain.shape)
    return (
        mixed_out,
        tokens_grad.reshape(tokens.shape),
        vectors[:slice_width],
        *qkv_w_grads,
        gain_grads[0],
        gain_grads[1],
        out_w_grad,
        vectors[slice_width : 2 * slice_width],
        router_grad,
        gate_w_grad,
        up_w_grad,
        down_grad,
    )


def solution(mesh):
    both = (SH, CT)
    rows = P(SH, CT, None, TS)
    pairs = P(SH, CT, None, None)
    vector, matrix, turned = P(both), P(both, TS), P(TS, both)
    up, down = P(both, None, TS), P(both, TS, None)
    return jax.shard_map(
        per_device,
        mesh=mesh,
        in_specs=(
            rows,
            P(SH, None),
            pairs,
            P(SH, CT, None),
            vector,
            matrix,
            matrix,
            matrix,
            turned,
            turned,
            turned,
            vector,
            P(both, None),
            up,
            up,
            down,
            rows,
        ),
        out_specs=(
            rows,
            rows,
            vector,
            matrix,
            matrix,
            matrix,
            turned,
            turned,
            turned,
            vector,
            P(both, None),
            up,
            up,
            down,
        ),
        check_vma=False,
    )
```
